32 devices in a mesh: segment: 2 (over core), seq: 8 (over z, x), mp: 2 (over y).
Axes of the slice: x: 2, y: 2, z: 4, core: 2. Of those that a mesh axis runs over, the one named last changes fastest.
Arguments:
- hidden: bfloat16 [2, 2, 1280, 2048], P('segment', None, 'seq', 'mp'), may hold values from -120 to 120
- memory: bfloat16 [2, 2, 1280, 2048], P('segment', None, 'seq', 'mp'), may hold values from -120 to 120
- w_query: bfloat16 [2, 2048, 2048], P('segment', None, 'mp'), may hold values from -1 to 1
- w_key: bfloat16 [2, 2048, 2048], P('segment', None, 'mp'), may hold values from -4 to 4
- w_value: bfloat16 [2, 2048, 2048], P('segment', None, 'mp'), may hold values from -0.125 to 0.125
- w_out: bfloat16 [2, 2048, 2048], P('segment', 'mp'), may hold values from -3 to 3
- norm_gain: float32 [2, 2048], P('segment'), may hold values from 0.1 to 1.9
- final_gain: float32 [2048], replicated, may hold values from 0.1 to 1.9
- lengths: int32 [2, 2, 2], P('segment'), may hold values from 640 to 1280, as said below
Outputs:
- sublayer: bfloat16 [2, 2, 1280, 2048], P('segment', None, 'seq', 'mp')
The draws below stay inside these ranges and needn't reach their ends.
Inputs may be any that keep to these rules, and one draw needn't show every extreme that they name: For each sequence b: lengths[0, b, 0] equals lengths[0, b, 1] (the encoder's document length); lengths[1, b, 0] is the target length and lengths[1, b, 1] the length of the document whose memory the decoder reads; one of these three lengths equals 1280.
All inputs are finite; a program needn't handle non-finite values.
Results may differ from the reference program's by a relative error of at most 0.018.
Values may be sent and summed in bfloat16 or wider, within the bound.
No kernel may reach another device: no remote copies, remote signals or barrier semaphores. Data moves between devices by JAX's collectives and lax.ppermute only.
A program may use at most 128 MiB of HBM per device.

```python
import math
import jax
import jax.numpy as jnp
from jax import lax

D = 2048
HEADS = 32
DH = 64
SEQS = 2
LEN = 1280


def states(seed_key):
    key_one = jax.random.fold_in(jax.random.fold_in(seed_key, 11), 0)
    key_three = jax.random.fold_in(jax.random.fold_in(seed_key, 11), 2)
    key_four = jax.random.fold_in(jax.random.fold_in(seed_key, 11), 3)
    full_shape = (3, SEQS, LEN, D)
    raw_draw = jnp.clip(jax.random.normal(key_one, full_shape, jnp.float32), -6.0, 6.0)
    row_scale = jnp.exp(jax.random.uniform(key_three, (3, SEQS, LEN, 1), jnp.float32, math.log(0.3), math.log(3.0)))
    col_scale = jnp.exp(jax.random.uniform(key_four, (3, 1, 1, D), jnp.float32, math.log(0.5), math.log(5.0)))
    drawn = raw_draw * row_scale * col_scale
    return jnp.clip(drawn, -120.0, 120.0)


def draw_hidden(key, part):
    drawn = states(key)
    return jnp.stack([drawn[0], drawn[1]]).astype(jnp.bfloat16)


def draw_memory(key, part):
    drawn = states(key)
    return jnp.stack([drawn[2], jnp.flip(drawn[2], axis=1)]).astype(jnp.bfloat16)


def query_key(seed_key):
    key_one, key_two = jax.random.split(jax.random.fold_in(seed_key, 23), 2)
    column_count = HEADS * DH
    full_shape = (2, D, column_count)
    weight_query = jnp.clip(jax.random.normal(key_one, full_shape, jnp.float32), -6.0, 6.0) / math.sqrt(D)
    weight_key = jnp.clip(jax.random.normal(key_two, full_shape, jnp.float32), -6.0, 6.0) / math.sqrt(D)
    return (weight_query, weight_key)


def draw_w_query(key, part):
    return query_key(key)[0].astype(jnp.bfloat16)


def draw_w_key(key, part):
    return query_key(key)[1].astype(jnp.bfloat16)


def draw_lengths(key, part):
    key_one, key_two = jax.random.split(jax.random.fold_in(key, 37), 2)
    drawn = jax.random.randint(key_one, (SEQS, 3), LEN // 2, LEN + 1)
    chosen = jax.random.randint(key_two, (SEQS, 1), 0, 3)
    drawn = jnp.where(jnp.arange(3)[None, :] == chosen, LEN, drawn)
    encoder_pair = jnp.stack([drawn[:, 0], drawn[:, 0]], axis=1)
    decoder_pair = jnp.stack([drawn[:, 1], drawn[:, 2]], axis=1)
    return jnp.stack([encoder_pair, decoder_pair]).astype(jnp.int32)


def steps_of(own_key, shape, cuts, least, high):
    def one(position, blocks):
        heights = jax.random.uniform(jax.random.fold_in(jax.random.fold_in(own_key, 6), position), (blocks,), jnp.float32, least / len(cuts), high / len(cuts))
        return jnp.repeat(jnp.exp(heights), shape[position] // blocks).reshape((-1,) + (1,) * (len(shape) - position - 1))

    level = one(*cuts[0])
    for cut in cuts[1:]:
        level = level * one(*cut)
    return level


def centred(stream_key, extent, deviation, bound, pieces=(), kind=jnp.bfloat16):
    array = jax.random.normal(stream_key, extent, jnp.float32) * deviation
    if len(pieces) > 0:
        array = steps_of(stream_key, extent, pieces, -0.22, 0.18) * array
    return jnp.clip(array, min=-bound, max=bound).astype(kind)


def setup_inputs(seed: int = 0) -> dict:
    key_of = jax.random.split(jax.random.key(seed), 10)
    hidden = draw_hidden(jax.random.fold_in(key_of[9], 71), 0)
    memory = draw_memory(jax.random.fold_in(key_of[9], 71), 0)
    w_query = draw_w_query(jax.random.fold_in(key_of[9], 71), 0)
    w_key = draw_w_key(jax.random.fold_in(key_of[9], 71), 0)
    w_value = centred(key_of[4], (2, D, HEADS * DH), D ** -0.5, 0.125, ((0, 2), (2, 2)))
    w_out = centred(key_of[5], (2, HEADS * DH, D), 0.5, 3.0, ((0, 2), (1, 2)))
    norm_gain = jnp.clip(1.0 + 0.18 * jax.random.normal(key_of[6], (2, D), jnp.float32), 0.1, 1.9)
    final_gain = jnp.clip(1.0 + 0.18 * jax.random.normal(key_of[7], (D,), jnp.float32), 0.1, 1.9)
    lengths = draw_lengths(jax.random.fold_in(key_of[9], 71), 0)
    return {"hidden": hidden, "memory": memory, "w_query": w_query, "w_key": w_key, "w_value": w_value, "w_out": w_out, "norm_gain": norm_gain, "final_gain": final_gain, "lengths": lengths}


def normalize(values, gain_row):
    widened = values.astype(jnp.float32)
    square = lax.optimization_barrier(jnp.mean(widened * widened, axis=-1, keepdims=True))
    return (widened * lax.rsqrt(square + 1e-06) * gain_row.astype(jnp.float32)).astype(jnp.bfloat16)

def attend_head(query_head, key_head, value_head, key_length):
    block_size = math.gcd(LEN, 1024)
    visible = jnp.arange(LEN) < key_length
    query_blocks = query_head.reshape(LEN // block_size, block_size, DH)

    def one_block(query_block):
        scores = jnp.dot(query_block, key_head.T, preferred_element_type=jnp.float32) * 0.25
        scores = jnp.where(visible[None, :], scores, -1e+30)
        largest = lax.optimization_barrier(jnp.max(scores, axis=-1, keepdims=True))
        exponent = jnp.where(visible[None, :], jnp.exp(scores - largest), 0.0)
        totals = lax.optimization_barrier(jnp.sum(exponent, axis=-1, keepdims=True))
        weighted = jnp.dot(exponent.astype(jnp.bfloat16), value_head, preferred_element_type=jnp.float32)
        return weighted / totals
    return lax.map(one_block, query_blocks).reshape(LEN, DH)

def section(query_src, key_src, query_gain, key_gain, weight_query, weight_key, weight_value, weight_out, length_pair):
    query_in = normalize(query_src, query_gain)
    key_in = normalize(key_src, key_gain)
    queries = jnp.dot(query_in, weight_query, preferred_element_type=jnp.float32).astype(jnp.bfloat16)
    keys = jnp.dot(key_in, weight_key, preferred_element_type=jnp.float32).astype(jnp.bfloat16)
    values = jnp.dot(key_in, weight_value, preferred_element_type=jnp.float32).astype(jnp.bfloat16)
    query_heads = queries.reshape(LEN, HEADS, DH).transpose(1, 0, 2)
    key_heads = keys.reshape(LEN, HEADS, DH).transpose(1, 0, 2)
    value_heads = values.reshape(LEN, HEADS, DH).transpose(1, 0, 2)
    key_length = length_pair[1]

    def per_head(triple):
        return attend_head(triple[0], triple[1], triple[2], key_length)
    context = lax.map(per_head, (query_heads, key_heads, value_heads))
    context = context.transpose(1, 0, 2).reshape(LEN, HEADS * DH)
    positions = jnp.arange(LEN)
    context = jnp.where((positions < length_pair[0])[:, None], context, 0.0).astype(jnp.bfloat16)
    branch = jnp.dot(context, weight_out, preferred_element_type=jnp.float32)
    return (query_src.astype(jnp.float32) + branch).astype(jnp.bfloat16)

def reference(hidden, memory, w_query, w_key, w_value, w_out, norm_gain, final_gain, lengths):
    encoder_out = jnp.stack([section(hidden[0, index], hidden[0, index], norm_gain[0], norm_gain[0], w_query[0], w_key[0], w_value[0], w_out[0], lengths[0, index]) for index in range(SEQS)])
    decoder_out = jnp.stack([section(hidden[1, index], memory[0, index], norm_gain[1], final_gain, w_query[1], w_key[1], w_value[1], w_out[1], lengths[1, index]) for index in range(SEQS)])
    return jnp.stack([encoder_out, decoder_out])
```

```python
import functools

import jax
import jax.numpy as jnp
from jax import lax
from jax.experimental import pallas as pl
from jax.experimental.pallas import tpu as pltpu
from jax.sharding import PartitionSpec as P

DH = 64
LANES = 128
SCALE = 0.25 * 1.4426950408889634
MIB = 1024 * 1024


def passed_along(value, axis, steps):
    count = lax.axis_size(axis)
    leading, last = (max(0, -steps), min(count, count - steps))
    return lax.ppermute(value, axis, [(source, source + steps) for source in range(leading, last)])


def normalize(values, gain_row):
    widened = values.astype(jnp.float32)
    square = jnp.mean(widened * widened, axis=-1, keepdims=True)
    return (widened * lax.rsqrt(square + 1e-06) * gain_row).astype(jnp.bfloat16)


def gathered_body(hidden, memory, w_query, w_key, w_value, w_out, norm_gain, final_gain, lengths):
    encoder_side = lax.axis_index("segment") == 0
    own_part = hidden[0]
    arrived = passed_along(memory[0], "segment", 1)
    source_part = jnp.where(encoder_side, own_part, arrived)
    query_rows, source_rows = (
        lax.all_gather(own_part, "mp", axis=2, tiled=True),
        lax.all_gather(source_part, "mp", axis=2, tiled=True),
    )
    batch = own_part.shape[0]
    row_count = own_part.shape[1]
    width = query_rows.shape[2]
    key_gain = jnp.where(encoder_side, norm_gain[0], final_gain)
    query_in = normalize(query_rows.reshape(batch * row_count, width), norm_gain[0])
    key_in = normalize(source_rows.reshape(batch * row_count, width), key_gain)
    head_cols = w_query.shape[2]
    local_heads = head_cols // DH
    queries = jnp.dot(query_in, w_query[0], preferred_element_type=jnp.float32).astype(jnp.bfloat16)
    keys = jnp.dot(key_in, w_key[0], preferred_element_type=jnp.float32).astype(jnp.bfloat16)
    values = jnp.dot(key_in, w_value[0], preferred_element_type=jnp.float32).astype(jnp.bfloat16)
    keys = keys.reshape(batch, row_count, head_cols)
    values = values.reshape(batch, row_count, head_cols)
    query_length = lengths[0, :, 0]
    key_length = lengths[0, :, 1]
    split_queries = queries.reshape(batch, row_count, local_heads, DH)
    key_piece = lax.all_gather(keys, "seq", axis=1, tiled=True)
    value_piece = lax.all_gather(values, "seq", axis=1, tiled=True)
    key_count = key_piece.shape[1]
    scores = (
        jnp.einsum(
            "bqhd,bkhd->bqhk",
            split_queries,
            key_piece.reshape(batch, key_count, local_heads, DH),
            preferred_element_type=jnp.float32,
        )
        * 0.25
    )
    visible = jnp.arange(key_count)[None, :] < key_length[:, None]
    mask = visible[:, None, None, :]
    scores = jnp.where(mask, scores, -1e30)
    largest = jnp.max(scores, axis=-1)
    exponent = jnp.where(mask, jnp.exp(scores - largest[..., None]), 0.0)
    totals = jnp.sum(exponent, axis=-1)
    weighted = jnp.einsum(
        "bqhk,bkhd->bqhd",
        exponent.astype(jnp.bfloat16),
        value_piece.reshape(batch, key_count, local_heads, DH),
        preferred_element_type=jnp.float32,
    )
    context = weighted / totals[..., None]
    positions = lax.axis_index("seq") * row_count + jnp.arange(row_count)
    live_rows = positions[None, :] < query_length[:, None]
    context = jnp.where(live_rows[:, :, None, None], context, 0.0)
    context = context.astype(jnp.bfloat16).reshape(batch * row_count, head_cols)
    partial_value = jnp.dot(context, w_out[0], preferred_element_type=jnp.float32)
    branch = lax.psum_scatter(
        partial_value.astype(jnp.bfloat16), "mp", scatter_dimension=1, tiled=True
    ).astype(jnp.float32)
    branch = branch.reshape(batch, row_count, branch.shape[1])
    return (own_part.astype(jnp.float32) + branch).astype(jnp.bfloat16)[None]


HEAD, SIDE, INNER, ENC = 0, 1, 2, 3
BLOCK = 4


def project_kernel(steps, table, qo, qn, ko, kn, gain, last_gain, wq, wk, wv, *rest):
    outs, (xq, xk) = rest[:steps], rest[steps:]
    step = pl.program_id(0)
    half = qo.shape[1]
    side = table[SIDE]

    @pl.when(step == 0)
    def _():
        encoder = table[ENC] == 1

        def fill(own, other, gains, into):
            a = own.astype(jnp.float32)
            b = other.astype(jnp.float32)
            square = jnp.sum(a * a, axis=-1, keepdims=True) + jnp.sum(b * b, axis=-1, keepdims=True)
            factor = lax.rsqrt(square / (2 * half) + 1e-06)
            into[0] = (a * factor * gains(side)).astype(jnp.bfloat16)
            into[1] = (b * factor * gains(1 - side)).astype(jnp.bfloat16)

        fill(qo[...], qn[...], lambda s: gain[pl.ds(s, 1), :], xq)

        @pl.when(encoder)
        def _():
            xk[...] = xq[...]

        @pl.when(jnp.logical_not(encoder))
        def _():
            fill(ko[...], kn[...], lambda s: last_gain[pl.ds(s, 1), :], xk)

    def rows(s):
        return pl.ds(pl.multiple_of(s * half, half), half)

    def times(x, w):
        total = jnp.dot(x[0], w[rows(side), :], preferred_element_type=jnp.float32)
        total += jnp.dot(x[1], w[rows(1 - side), :], preferred_element_type=jnp.float32)
        return total.astype(jnp.bfloat16)

    width = wq.shape[1]
    products = [times(xq, wq), times(xk, wk), times(xk, wv)]
    for i in range(steps):

        @pl.when(step == i)
        def _(i=i):
            for place, product in enumerate(products):
                outs[i][:, place * width : (place + 1) * width] = product


def project(table, turns, qo, qn, ko, kn, gain, last_gain, wq, wk, wv, width):
    rows, half = qo.shape
    steps = len(turns)

    def weight_block(i, table):
        turn = sum((jnp.where(i == n, t, 0) for n, t in enumerate(turns)), 0)
        return (0, table[HEAD] ^ turn)

    whole = lambda i, table: (0, 0)
    part = pl.BlockSpec((rows, half), whole)
    gains = pl.BlockSpec((2, half), whole)
    weight = pl.BlockSpec((2 * half, width), weight_block)
    return pl.pallas_call(
        functools.partial(project_kernel, steps),
        out_shape=[jax.ShapeDtypeStruct((rows, 3 * width), jnp.bfloat16)] * steps,
        grid_spec=pltpu.PrefetchScalarGridSpec(
            num_scalar_prefetch=1,
            grid=(steps,),
            in_specs=[part] * 4 + [gains] * 2 + [weight] * 3,
            out_specs=[pl.BlockSpec((rows, 3 * width), whole)] * steps,
            scratch_shapes=[pltpu.VMEM((2, rows, half), jnp.bfloat16)] * 2,
        ),
        compiler_params=pltpu.CompilerParams(vmem_limit_bytes=24 * MIB),
        cost_estimate=pl.CostEstimate(
            flops=2 * rows * 2 * half * 3 * width * steps,
            bytes_accessed=2 * (4 * rows * half + 6 * half * width * steps + rows * 3 * width * steps),
            transcendentals=0,
        ),
    )(table, qo, qn, ko, kn, gain, last_gain, wq, wk, wv)


def attend_kernel(blocks, table, lengths, *refs):
    q_refs, k_refs, v_refs = refs[:blocks], refs[blocks : 2 * blocks], refs[2 * blocks : 3 * blocks]
    outs = refs[3 * blocks : 3 * blocks + blocks // 2]
    qs, ks, vs = refs[3 * blocks + blocks // 2 :]
    rows = q_refs[0].shape[0]
    key_length = lengths[2 * table[INNER] + 1]
    query_length = lengths[2 * table[INNER]]
    lane = lax.broadcasted_iota(jnp.int32, (rows, LANES), 1)
    low = lane < DH
    row = lax.broadcasted_iota(jnp.int32, (rows, LANES), 0)
    zero = jnp.zeros((rows, LANES), jnp.bfloat16)
    one = jnp.ones((rows, LANES), jnp.bfloat16)
    unit = jnp.where(lane == 0, one, zero)
    for j in range(blocks):
        here = pl.ds(j * rows, rows)
        qs[here, :LANES] = q_refs[j][...]
        qs[here, LANES:] = unit
        key = k_refs[j][...]
        hides = jnp.logical_and(lane == 0, row + table[BLOCK + j] >= key_length)
        bias = jnp.where(hides, -1e30, 0.0).astype(jnp.bfloat16)
        value = v_refs[j][...]
        ks[0, here, :LANES] = jnp.where(low, key, zero)
        ks[1, here, :LANES] = jnp.where(low, zero, key)
        ks[0, here, LANES:] = bias
        ks[1, here, LANES:] = bias
        vs[0, here, :] = jnp.where(low, value, one)
        vs[1, here, :] = jnp.where(low, one, value)

    for j in range(blocks):
        query = qs[pl.ds(j * rows, rows), :]
        sums = []
        for head in range(2):
            scores = lax.dot_general(
                query, ks[head], (((1,), (1,)), ((), ())), preferred_element_type=jnp.float32
            )
            largest = jnp.max(scores, axis=-1, keepdims=True)
            weights = jnp.exp2((scores - largest) * SCALE).astype(jnp.bfloat16)
            sums.append(jnp.dot(weights, vs[head], preferred_element_type=jnp.float32))
        weighted = jnp.where(low, sums[0], sums[1])
        totals = jnp.where(low, pltpu.roll(sums[0], DH, 1), pltpu.roll(sums[1], DH, 1))
        live = row + table[BLOCK + j] < query_length
        context = jnp.where(live, weighted / totals, 0.0).astype(jnp.bfloat16)
        outs[j // 2][pl.ds((j % 2) * rows, rows), :] = context


def attend(table, lengths, parts, pair, pairs):
    blocks = len(parts)
    rows = parts[0].shape[0]
    count = blocks * rows

    def column(place):
        return pl.BlockSpec((rows, LANES), lambda i, table, lengths: (0, place * pairs + pair))

    return pl.pallas_call(
        functools.partial(attend_kernel, blocks),
        out_shape=[jax.ShapeDtypeStruct((2 * rows, LANES), jnp.bfloat16)] * (blocks // 2),
        grid_spec=pltpu.PrefetchScalarGridSpec(
            num_scalar_prefetch=2,
            grid=(1,),
            in_specs=[column(0)] * blocks + [column(1)] * blocks + [column(2)] * blocks,
            out_specs=[pl.BlockSpec((2 * rows, LANES), lambda i, table, lengths: (0, 0))] * (blocks // 2),
            scratch_shapes=[
                pltpu.VMEM((count, 2 * LANES), jnp.bfloat16),
                pltpu.VMEM((2, count, 2 * LANES), jnp.bfloat16),
                pltpu.VMEM((2, count, LANES), jnp.bfloat16),
            ],
        ),
        compiler_params=pltpu.CompilerParams(vmem_limit_bytes=32 * MIB),
        cost_estimate=pl.CostEstimate(
            flops=4 * count * count * 2 * LANES,
            bytes_accessed=8 * count * LANES,
            transcendentals=2 * count * count,
        ),
    )(table, lengths, *parts, *parts, *parts)


def output_kernel(count, pairs, table, w, *refs):
    pieces, (first, second), x = refs[: count * pairs], refs[count * pairs : count * pairs + 2], refs[-1]
    for turn in range(count):
        for pair in range(pairs):
            place = (table[HEAD] ^ turn) * pairs + pair
            x[:, pl.ds(pl.multiple_of(place * LANES, LANES), LANES)] = pieces[turn * pairs + pair][...]
    total = jnp.dot(x[...], w[...], preferred_element_type=jnp.float32).astype(jnp.bfloat16)
    rows = first.shape[0]
    first[...] = total[:rows]
    second[...] = total[rows:]


def output_part(table, pieces, w_out, count, pairs, own):
    rows, depth, half = pieces[0].shape[0] // 2, w_out.shape[0], w_out.shape[1] // 2

    def weight_block(i, table):
        return (0, table[SIDE] if own else 1 - table[SIDE])

    return pl.pallas_call(
        functools.partial(output_kernel, count, pairs),
        out_shape=[jax.ShapeDtypeStruct((rows, half), jnp.bfloat16)] * 2,
        grid_spec=pltpu.PrefetchScalarGridSpec(
            num_scalar_prefetch=1,
            grid=(1,),
            in_specs=[pl.BlockSpec((depth, half), weight_block)]
            + [pl.BlockSpec((2 * rows, LANES), lambda i, table: (0, 0))] * (count * pairs),
            out_specs=[pl.BlockSpec((rows, half), lambda i, table: (0, 0))] * 2,
            scratch_shapes=[pltpu.VMEM((2 * rows, depth), jnp.bfloat16)],
        ),
        compiler_params=pltpu.CompilerParams(vmem_limit_bytes=24 * MIB),
        cost_estimate=pl.CostEstimate(
            flops=4 * rows * depth * half,
            bytes_accessed=2 * (depth * half + 2 * rows * depth + 2 * rows * half),
            transcendentals=0,
        ),
    )(table, w_out, *pieces)


def add_kernel(table, hidden, own, beside, across, corner, out):
    def total(a, b):
        out[0, 0] = (
            hidden[0, 0].astype(jnp.float32) + (a[...].astype(jnp.float32) + b[...].astype(jnp.float32))
        ).astype(jnp.bfloat16)

    @pl.when(pl.program_id(0) == 0)
    def _():
        total(own, beside)

    @pl.when(pl.program_id(0) == 1)
    def _():
        total(across, corner)


def add_all(table, hidden, own, beside, across, corner):
    rows, half = own.shape
    block = pl.BlockSpec((1, 1, rows, half), lambda i, table: (0, table[INNER] ^ i, 0, 0))
    part = pl.BlockSpec((rows, half), lambda i, table: (0, 0))
    return pl.pallas_call(
        add_kernel,
        out_shape=jax.ShapeDtypeStruct(hidden.shape, jnp.bfloat16),
        grid_spec=pltpu.PrefetchScalarGridSpec(
            num_scalar_prefetch=1,
            grid=(2,),
            in_specs=[block, part, part, part, part],
            out_specs=block,
        ),
        compiler_params=pltpu.CompilerParams(vmem_limit_bytes=16 * MIB),
    )(table, hidden, own, beside, across, corner)


def body(hidden, memory, w_query, w_key, w_value, w_out, norm_gain, final_gain, lengths):
    seq, mp = lax.axis_size("seq"), lax.axis_size("mp")
    count = seq // 2
    rows, half = hidden.shape[2:]
    width = w_query.shape[2] // count
    pairs = width // LANES

    place, side = lax.axis_index("seq"), lax.axis_index("mp")
    outer, inner = place // 2, place % 2
    encoder = (lax.axis_index("segment") == 0).astype(jnp.int32)
    starts = [
        (2 * (outer ^ turn) + (inner ^ chunk)) * rows for turn in range(count) for chunk in range(2)
    ]
    table = jnp.stack([outer, side, inner, encoder] + starts).astype(jnp.int32)

    def moved(value, swap_seq, swap_mp):
        pairs = [
            (s * mp + m, (s ^ swap_seq) * mp + (m ^ swap_mp)) for s in range(seq) for m in range(mp)
        ]
        return lax.ppermute(value, ("seq", "mp"), pairs)

    def handed(value, swap_seq, swap_mp):
        pairs = [
            (s * mp + m, seq * mp + (s ^ swap_seq) * mp + (m ^ swap_mp)) for s in range(seq) for m in range(mp)
        ]
        return lax.ppermute(value, ("segment", "seq", "mp"), pairs)

    def turned(value, turn):
        return lax.ppermute(value, "seq", [(s, s ^ (2 * turn)) for s in range(seq)])

    hidden_own = lax.dynamic_index_in_dim(hidden[0], inner, 0, keepdims=False)
    hidden_away = lax.dynamic_index_in_dim(hidden[0], 1 - inner, 0, keepdims=False)
    memory_own = lax.dynamic_index_in_dim(memory[0], inner, 0, keepdims=False)
    memory_away = lax.dynamic_index_in_dim(memory[0], 1 - inner, 0, keepdims=False)

    query_beside = moved(hidden_own, 0, 1)
    source_beside = handed(memory_own, 0, 1)
    source_here = handed(memory_own, 0, 0)
    query_corner = moved(hidden_away, 1, 1)
    source_corner = handed(memory_away, 1, 1)
    query_across = moved(hidden_away, 1, 0)
    source_across = handed(memory_away, 1, 0)

    gain = norm_gain[0].reshape(2, half)
    last_gain = final_gain.reshape(2, half)
    weights = (w_query[0], w_key[0], w_value[0])
    turns = tuple(range(count - 1, -1, -1))
    chunks = []
    for qo, qn, ko, kn in (
        (hidden_own, query_beside, source_here, source_beside),
        (query_across, query_corner, source_across, source_corner),
    ):
        products = project(table, turns, qo, qn, ko, kn, gain, last_gain, *weights, width)
        chunks.append({t: turned(p, t) if t else p for t, p in zip(turns, products)})
    parts = [chunks[chunk][turn] for turn in range(count) for chunk in range(2)]

    pieces = [[None] * pairs for _ in range(count)]
    for pair in range(pairs):
        contexts = attend(table, lengths.reshape(-1), parts, pair, pairs)
        for turn in turns:
            pieces[turn][pair] = turned(contexts[turn], turn) if turn else contexts[turn]
    flat = [piece for row in pieces for piece in row]

    beside, corner = output_part(table, flat, w_out[0], count, pairs, False)
    corner = moved(corner, 1, 1)
    beside = moved(beside, 0, 1)
    own, across = output_part(table, flat, w_out[0], count, pairs, True)
    across = moved(across, 1, 0)
    return add_all(table, hidden, own, beside, across, corner)


def solution(mesh):
    seq, mp = mesh.shape["seq"], mesh.shape["mp"]

    def chosen(*arrays):
        batch, columns = arrays[0].shape[1], arrays[2].shape[2]
        count = seq // 2
        fits = (
            batch == 2
            and mp == 2
            and seq % 2 == 0
            and count & (count - 1) == 0
            and (columns // mp) % (count * LANES) == 0
            and (arrays[0].shape[2] // seq) % 16 == 0
        )
        return jax.shard_map(
            body if fits else gathered_body,
            mesh=mesh,
            in_specs=(
                P("segment", None, "seq", "mp"),
                P("segment", None, "seq", "mp"),
                P("segment", None, "mp"),
                P("segment", None, "mp"),
                P("segment", None, "mp"),
                P("segment", "mp", None),
                P("segment", None),
                P(),
                P("segment", None, None),
            ),
            out_specs=P("segment", None, "seq", "mp"),
            check_vma=False,
        )(*arrays)

    return chosen
```

```python
import functools

import jax
import jax.numpy as jnp
from jax import lax
from jax.experimental import pallas as pl
from jax.experimental.pallas import tpu as pltpu
from jax.sharding import PartitionSpec as P

DH = 64
LANES = 128
SCALE = 0.25 * 1.4426950408889634
MIB = 1024 * 1024


def passed_along(value, axis, steps):
    count = lax.axis_size(axis)
    leading, last = (max(0, -steps), min(count, count - steps))
    return lax.ppermute(value, axis, [(source, source + steps) for source in range(leading, last)])


def normalize(values, gain_row):
    widened = values.astype(jnp.float32)
    square = jnp.mean(widened * widened, axis=-1, keepdims=True)
    return (widened * lax.rsqrt(square + 1e-06) * gain_row).astype(jnp.bfloat16)


def gathered_body(hidden, memory, w_query, w_key, w_value, w_out, norm_gain, final_gain, lengths):
    encoder_side = lax.axis_index("segment") == 0
    own_part = hidden[0]
    arrived = passed_along(memory[0], "segment", 1)
    source_part = jnp.where(encoder_side, own_part, arrived)
    query_rows, source_rows = (
        lax.all_gather(own_part, "mp", axis=2, tiled=True),
        lax.all_gather(source_part, "mp", axis=2, tiled=True),
    )
    batch = own_part.shape[0]
    row_count = own_part.shape[1]
    width = query_rows.shape[2]
    key_gain = jnp.where(encoder_side, norm_gain[0], final_gain)
    query_in = normalize(query_rows.reshape(batch * row_count, width), norm_gain[0])
    key_in = normalize(source_rows.reshape(batch * row_count, width), key_gain)
    head_cols = w_query.shape[2]
    local_heads = head_cols // DH
    queries = jnp.dot(query_in, w_query[0], preferred_element_type=jnp.float32).astype(jnp.bfloat16)
    keys = jnp.dot(key_in, w_key[0], preferred_element_type=jnp.float32).astype(jnp.bfloat16)
    values = jnp.dot(key_in, w_value[0], preferred_element_type=jnp.float32).astype(jnp.bfloat16)
    keys = keys.reshape(batch, row_count, head_cols)
    values = values.reshape(batch, row_count, head_cols)
    query_length = lengths[0, :, 0]
    key_length = lengths[0, :, 1]
    split_queries = queries.reshape(batch, row_count, local_heads, DH)
    key_piece = lax.all_gather(keys, "seq", axis=1, tiled=True)
    value_piece = lax.all_gather(values, "seq", axis=1, tiled=True)
    key_count = key_piece.shape[1]
    scores = (
        jnp.einsum(
            "bqhd,bkhd->bqhk",
            split_queries,
            key_piece.reshape(batch, key_count, local_heads, DH),
            preferred_element_type=jnp.float32,
        )
        * 0.25
    )
    visible = jnp.arange(key_count)[None, :] < key_length[:, None]
    mask = visible[:, None, None, :]
    scores = jnp.where(mask, scores, -1e30)
    largest = jnp.max(scores, axis=-1)
    exponent = jnp.where(mask, jnp.exp(scores - largest[..., None]), 0.0)
    totals = jnp.sum(exponent, axis=-1)
    weighted = jnp.einsum(
        "bqhk,bkhd->bqhd",
        exponent.astype(jnp.bfloat16),
        value_piece.reshape(batch, key_count, local_heads, DH),
        preferred_element_type=jnp.float32,
    )
    context = weighted / totals[..., None]
    positions = lax.axis_index("seq") * row_count + jnp.arange(row_count)
    live_rows = positions[None, :] < query_length[:, None]
    context = jnp.where(live_rows[:, :, None, None], context, 0.0)
    context = context.astype(jnp.bfloat16).reshape(batch * row_count, head_cols)
    partial_value = jnp.dot(context, w_out[0], preferred_element_type=jnp.float32)
    branch = lax.psum_scatter(
        partial_value.astype(jnp.bfloat16), "mp", scatter_dimension=1, tiled=True
    ).astype(jnp.float32)
    branch = branch.reshape(batch, row_count, branch.shape[1])
    return (own_part.astype(jnp.float32) + branch).astype(jnp.bfloat16)[None]


HEAD, SIDE, INNER, ENC = 0, 1, 2, 3
BLOCK = 4


def in_hbm(array):
    return pltpu.with_memory_space_constraint(array, pltpu.HBM)


def times_gain(values, gains, side, into):
    half = values.shape[1]
    wide = values.astype(jnp.float32)
    into[...] = (wide * gains[:, pl.ds(pl.multiple_of(side * half, half), half)]).astype(jnp.bfloat16)
    return jnp.sum(wide * wide, axis=-1, keepdims=True)


def start_weights(weights, halves, held, sems, parts):
    half = held.shape[2]
    size = half // parts
    copies = [[] for _ in weights]
    for n, weight in enumerate(weights):
        for h, side in enumerate(halves):
            for m in range(parts):
                source = pl.ds(pl.multiple_of(side * half + m * size, size), size)
                copy = pltpu.make_async_copy(
                    weight.at[0, source], held.at[n, h, pl.ds(m * size, size)], sems.at[n, h, m]
                )
                copy.start()
                copies[n].append(copy)
    return copies


def begin_kernel(parts, table, hidden, memory, gain, last_gain, wk, wv, wq, ak, av, aq, sk, sq, xk, xq, held, sems):
    side = table[SIDE]
    copies = start_weights((wk, wv, wq), (side,), held, sems, parts)
    encoder = table[ENC] == 1
    total = times_gain(hidden[...], gain, side, xq)
    sq[...] = jnp.broadcast_to(total, sq.shape)

    @pl.when(encoder)
    def _():
        xk[...] = xq[...]
        sk[...] = sq[...]

    @pl.when(jnp.logical_not(encoder))
    def _():
        total = times_gain(memory[0], last_gain, side, xk)
        sk[...] = jnp.broadcast_to(total, sk.shape)

    for n, (x, out) in enumerate(((xk, ak), (xk, av), (xq, aq))):
        for copy in copies[n]:
            copy.wait()
        out[...] = jnp.dot(x[...], held[n, 0], preferred_element_type=jnp.float32)


def begin(table, hidden, memory, gains, weights, parts=4):
    rows, half = hidden.shape
    columns = weights[0].shape[2]
    whole = lambda i, table: (0, 0)
    shares, squares = ((rows, columns), (rows, LANES))
    return pl.pallas_call(
        functools.partial(begin_kernel, parts),
        out_shape=[jax.ShapeDtypeStruct(shape, jnp.float32) for shape in [shares] * 3 + [squares] * 2],
        grid_spec=pltpu.PrefetchScalarGridSpec(
            num_scalar_prefetch=1,
            grid=(1,),
            in_specs=[
                pl.BlockSpec((rows, half), whole),
                pl.BlockSpec((1, rows, half), lambda i, table: (table[INNER], 0, 0)),
            ]
            + [pl.BlockSpec((1, 2 * half), whole)] * 2
            + [pl.BlockSpec(memory_space=pltpu.HBM)] * 3,
            out_specs=[pl.BlockSpec(shape, whole) for shape in [shares] * 3 + [squares] * 2],
            scratch_shapes=[pltpu.VMEM((rows, half), jnp.bfloat16)] * 2
            + [pltpu.VMEM((3, 1, half, columns), jnp.bfloat16), pltpu.SemaphoreType.DMA((3, 1, parts))],
        ),
        compiler_params=pltpu.CompilerParams(vmem_limit_bytes=24 * MIB),
        cost_estimate=pl.CostEstimate(
            flops=6 * rows * half * columns, bytes_accessed=6 * half * columns, transcendentals=0
        ),
    )(table, hidden, memory, *gains, *[in_hbm(w) for w in weights])


def end_kernel(parts, count, table, qn, kn, gain, last_gain, wk, wv, wq, ak, av, aq, sk, sq, *rest):
    outs, (xk, xq, fk, fq, held, sems) = rest[: 2 * count], rest[2 * count :]
    side = 1 - table[SIDE]
    features = 2 * qn.shape[1]
    width = outs[count].shape[1]
    copies = start_weights((wk, wv, wq), (side,), held, sems, parts)
    encoder = table[ENC] == 1

    def factor(total):
        return lax.rsqrt(total / features + 1e-06)

    fq[...] = factor(sq[...] + times_gain(qn[...], gain, side, xq))

    @pl.when(encoder)
    def _():
        xk[...] = xq[...]
        fk[...] = fq[...]

    @pl.when(jnp.logical_not(encoder))
    def _():
        fk[...] = factor(sk[...] + times_gain(kn[...], last_gain, side, xk))

    for n, (x, share, f) in enumerate(((xk, ak, fk), (xk, av, fk), (xq, aq, fq))):
        for copy in copies[n]:
            copy.wait()
        scale = f[:, :1] * SCALE if n == 2 else f[:, :1]
        for turn in range(count):
            columns = pl.ds(pl.multiple_of((table[HEAD] ^ turn) * width, width), width)
            total = share[:, columns] + jnp.dot(x[...], held[n, 0, :, columns], preferred_element_type=jnp.float32)
            total = (total * scale).astype(jnp.bfloat16)
            if n == 2:
                outs[count + turn][...] = total
            else:
                outs[turn][:, n * width : (n + 1) * width] = total


def end(table, qn, kn, gains, weights, shares, count, parts=4):
    rows, half = qn.shape
    columns = weights[0].shape[2]
    width = columns // count
    whole = lambda i, table: (0, 0)
    widths = [2 * width] * count + [width] * count
    return pl.pallas_call(
        functools.partial(end_kernel, parts, count),
        out_shape=[jax.ShapeDtypeStruct((rows, w), jnp.bfloat16) for w in widths],
        grid_spec=pltpu.PrefetchScalarGridSpec(
            num_scalar_prefetch=1,
            grid=(1,),
            in_specs=[pl.BlockSpec((rows, half), whole)] * 2
            + [pl.BlockSpec((1, 2 * half), whole)] * 2
            + [pl.BlockSpec(memory_space=pltpu.HBM)] * 3
            + [pl.BlockSpec((rows, columns), whole)] * 3
            + [pl.BlockSpec((rows, LANES), whole)] * 2,
            out_specs=[pl.BlockSpec((rows, w), whole) for w in widths],
            scratch_shapes=[pltpu.VMEM((rows, half), jnp.bfloat16)] * 2
            + [pltpu.VMEM((rows, LANES), jnp.float32)] * 2
            + [pltpu.VMEM((3, 1, half, columns), jnp.bfloat16), pltpu.SemaphoreType.DMA((3, 1, parts))],
        ),
        compiler_params=pltpu.CompilerParams(vmem_limit_bytes=24 * MIB),
        cost_estimate=pl.CostEstimate(
            flops=6 * rows * half * columns, bytes_accessed=6 * half * columns, transcendentals=0
        ),
    )(table, qn, kn, *gains, *[in_hbm(w) for w in weights], *shares)


def project_kernel(parts, count, table, qo, qn, ko, kn, gain, last_gain, wk, wv, wq, *rest):
    outs, (xk, xq, fk, fq, held, sems) = rest[:count], rest[count:]
    side = table[SIDE]
    features = 2 * qn.shape[1]
    width = outs[0].shape[1] // 3
    copies = start_weights((wk, wv, wq), (side, 1 - side), held, sems, parts)
    encoder = table[ENC] == 1

    def fill(own, other, gains, x, f):
        total = times_gain(own[...], gains, side, x.at[0]) + times_gain(other[...], gains, 1 - side, x.at[1])
        f[...] = jnp.broadcast_to(lax.rsqrt(total / features + 1e-06), f.shape)

    fill(qo, qn, gain, xq, fq)

    @pl.when(encoder)
    def _():
        xk[...] = xq[...]
        fk[...] = fq[...]

    @pl.when(jnp.logical_not(encoder))
    def _():
        fill(ko, kn, last_gain, xk, fk)

    for n, (x, f) in enumerate(((xk, fk), (xk, fk), (xq, fq))):
        for copy in copies[n]:
            copy.wait()
        scale = f[:, :1] * SCALE if n == 2 else f[:, :1]
        for turn in range(count):
            columns = pl.ds(pl.multiple_of((table[HEAD] ^ turn) * width, width), width)
            total = jnp.dot(x[0], held[n, 0, :, columns], preferred_element_type=jnp.float32)
            total += jnp.dot(x[1], held[n, 1, :, columns], preferred_element_type=jnp.float32)
            outs[turn][:, n * width : (n + 1) * width] = (total * scale).astype(jnp.bfloat16)


def project(table, qo, qn, ko, kn, gains, weights, count, parts=4):
    rows, half = qo.shape
    columns = weights[0].shape[2]
    width = 3 * columns // count
    whole = lambda i, table: (0, 0)
    return pl.pallas_call(
        functools.partial(project_kernel, parts, count),
        out_shape=[jax.ShapeDtypeStruct((rows, width), jnp.bfloat16)] * count,
        grid_spec=pltpu.PrefetchScalarGridSpec(
            num_scalar_prefetch=1,
            grid=(1,),
            in_specs=[pl.BlockSpec((rows, half), whole)] * 4
            + [pl.BlockSpec((1, 2 * half), whole)] * 2
            + [pl.BlockSpec(memory_space=pltpu.HBM)] * 3,
            out_specs=[pl.BlockSpec((rows, width), whole)] * count,
            scratch_shapes=[pltpu.VMEM((2, rows, half), jnp.bfloat16)] * 2
            + [pltpu.VMEM((rows, LANES), jnp.float32)] * 2
            + [pltpu.VMEM((3, 2, half, columns), jnp.bfloat16), pltpu.SemaphoreType.DMA((3, 2, parts))],
        ),
        compiler_params=pltpu.CompilerParams(vmem_limit_bytes=32 * MIB),
        cost_estimate=pl.CostEstimate(
            flops=12 * rows * half * columns, bytes_accessed=12 * half * columns, transcendentals=0
        ),
    )(table, qo, qn, ko, kn, *gains, *[in_hbm(w) for w in weights])


def attend_kernel(count, chunk, tile, table, lengths, *refs):
    q_refs, k_refs, v_refs = refs[:count], refs[count : 3 * count], refs[3 * count : 5 * count]
    outs, (qs, ks, vs, contexts) = refs[5 * count : 6 * count], refs[6 * count :]
    rows, width = q_refs[0].shape
    pairs = width // LANES
    query_length = lengths[2 * table[INNER]]
    key_length = lengths[2 * table[INNER] + 1]
    lane = lax.broadcasted_iota(jnp.int32, (rows, LANES), 1)
    row = lax.broadcasted_iota(jnp.int32, (rows, LANES), 0)
    low = lane < DH
    zero = jnp.zeros((rows, LANES), jnp.bfloat16)
    one = jnp.ones((rows, LANES), jnp.bfloat16)
    unit = jnp.where(lane == 0, one, zero)
    for j in range(2 * count):
        here = pl.ds(j * rows, rows)
        hides = jnp.logical_and(lane == 0, row + table[BLOCK + j] >= key_length)
        bias = jnp.where(hides, -1e30, 0.0).astype(jnp.bfloat16)
        for pair in range(pairs):
            columns = slice(pair * LANES, (pair + 1) * LANES)
            key = k_refs[j][:, columns]
            value = v_refs[j][:, columns]
            ks[pair, 0, here, :LANES] = jnp.where(low, key, zero)
            ks[pair, 1, here, :LANES] = jnp.where(low, zero, key)
            ks[pair, 0, here, LANES:] = bias
            ks[pair, 1, here, LANES:] = bias
            vs[pair, 0, here, :] = jnp.where(low, value, one)
            vs[pair, 1, here, :] = jnp.where(low, one, value)
    for j in range(count):
        here = pl.ds(j * rows, rows)
        for pair in range(pairs):
            qs[pair, here, :LANES] = q_refs[j][:, pair * LANES : (pair + 1) * LANES]
            qs[pair, here, LANES:] = unit

    low = lax.broadcasted_iota(jnp.int32, (tile, LANES), 1) < DH
    for pair in range(pairs):
        for t in range(count * rows // tile):
            query = qs[pair, pl.ds(t * tile, tile), :]
            sums = []
            for head in range(2):
                scores = lax.dot_general(
                    query, ks[pair, head], (((1,), (1,)), ((), ())), preferred_element_type=jnp.float32
                )
                largest = jnp.max(scores, axis=-1, keepdims=True)
                weights = jnp.exp2(scores - largest).astype(jnp.bfloat16)
                sums.append(jnp.dot(weights, vs[pair, head], preferred_element_type=jnp.float32))
            weighted = jnp.where(low, sums[0], sums[1])
            totals = jnp.where(low, pltpu.roll(sums[0], DH, 1), pltpu.roll(sums[1], DH, 1))
            contexts[pl.ds(t * tile, tile), pair * LANES : (pair + 1) * LANES] = (weighted / totals).astype(
                jnp.bfloat16
            )

    for j in range(count):
        live = row + table[BLOCK + 2 * j + chunk] < query_length
        for pair in range(pairs):
            columns = slice(pair * LANES, (pair + 1) * LANES)
            outs[j][:, columns] = jnp.where(live, contexts[pl.ds(j * rows, rows), columns], zero)


def attend(table, lengths, queries, keyed, chunk, width):
    count = len(queries)
    rows = queries[0][0].shape[0]
    total = 2 * count * rows

    def column(place):
        return pl.BlockSpec((rows, width), lambda i, table, lengths: (0, place))

    return pl.pallas_call(
        functools.partial(attend_kernel, count, chunk, 2 * rows if count % 2 == 0 else rows),
        out_shape=[jax.ShapeDtypeStruct((rows, width), jnp.bfloat16)] * count,
        grid_spec=pltpu.PrefetchScalarGridSpec(
            num_scalar_prefetch=2,
            grid=(1,),
            in_specs=[column(place) for _, place in queries] + [column(0)] * (2 * count) + [column(1)] * (2 * count),
            out_specs=[column(0)] * count,
            scratch_shapes=[
                pltpu.VMEM((width // LANES, count * rows, 2 * LANES), jnp.bfloat16),
                pltpu.VMEM((width // LANES, 2, total, 2 * LANES), jnp.bfloat16),
                pltpu.VMEM((width // LANES, 2, total, LANES), jnp.bfloat16),
                pltpu.VMEM((count * rows, width), jnp.bfloat16),
            ],
        ),
        compiler_params=pltpu.CompilerParams(vmem_limit_bytes=32 * MIB),
        cost_estimate=pl.CostEstimate(
            flops=4 * count * rows * total * 2 * width,
            bytes_accessed=6 * total * width,
            transcendentals=count * rows * total * (width // DH),
        ),
    )(table, lengths, *[array for array, _ in queries], *keyed, *keyed)


def output_kernel(count, table, w, *refs):
    pieces, outs, x = refs[:count], refs[count : count + 2], refs[-1]
    step = pl.program_id(0)
    width = pieces[0].shape[1]

    @pl.when(step == 0)
    def _():
        for turn in range(count):
            place = pl.multiple_of((table[HEAD] ^ turn) * width, width)
            x[:, pl.ds(place, width)] = pieces[turn][...]

    total = jnp.dot(x[...], w[...], preferred_element_type=jnp.float32).astype(jnp.bfloat16)
    for i in range(2):

        @pl.when(step == i)
        def _(i=i):
            outs[i][...] = total


def output_parts(table, pieces, w_out):
    rows, width = pieces[0].shape
    depth, half = w_out.shape[0], w_out.shape[1] // 2
    whole = lambda i, table: (0, 0)
    return pl.pallas_call(
        functools.partial(output_kernel, len(pieces)),
        out_shape=[jax.ShapeDtypeStruct((rows, half), jnp.bfloat16)] * 2,
        grid_spec=pltpu.PrefetchScalarGridSpec(
            num_scalar_prefetch=1,
            grid=(2,),
            in_specs=[pl.BlockSpec((depth, half), lambda i, table: (0, 1 - (table[SIDE] ^ i)))]
            + [pl.BlockSpec((rows, width), whole)] * len(pieces),
            out_specs=[pl.BlockSpec((rows, half), whole)] * 2,
            scratch_shapes=[pltpu.VMEM((rows, depth), jnp.bfloat16)],
        ),
        compiler_params=pltpu.CompilerParams(vmem_limit_bytes=24 * MIB),
        cost_estimate=pl.CostEstimate(
            flops=4 * rows * depth * half,
            bytes_accessed=2 * (2 * depth * half + rows * depth + 2 * rows * half),
            transcendentals=0,
        ),
    )(table, w_out, *pieces)


def add_kernel(table, hidden, own, beside, across, corner, out):
    def total(a, b):
        out[0, 0] = (
            hidden[0, 0].astype(jnp.float32) + (a[...].astype(jnp.float32) + b[...].astype(jnp.float32))
        ).astype(jnp.bfloat16)

    @pl.when(pl.program_id(0) == 0)
    def _():
        total(own, beside)

    @pl.when(pl.program_id(0) == 1)
    def _():
        total(across, corner)


def add_all(table, hidden, own, beside, across, corner):
    rows, half = own.shape
    block = pl.BlockSpec((1, 1, rows, half), lambda i, table: (0, table[INNER] ^ i, 0, 0))
    part = pl.BlockSpec((rows, half), lambda i, table: (0, 0))
    return pl.pallas_call(
        add_kernel,
        out_shape=jax.ShapeDtypeStruct(hidden.shape, jnp.bfloat16),
        grid_spec=pltpu.PrefetchScalarGridSpec(
            num_scalar_prefetch=1,
            grid=(2,),
            in_specs=[block, part, part, part, part],
            out_specs=block,
        ),
        compiler_params=pltpu.CompilerParams(vmem_limit_bytes=16 * MIB),
    )(table, hidden, own, beside, across, corner)


def body(hidden, memory, w_query, w_key, w_value, w_out, norm_gain, final_gain, lengths):
    seq, mp = lax.axis_size("seq"), lax.axis_size("mp")
    count = seq // 2
    rows, half = hidden.shape[2:]
    width = w_query.shape[2] // count

    place, side = lax.axis_index("seq"), lax.axis_index("mp")
    outer, inner = place // 2, place % 2
    encoder = (lax.axis_index("segment") == 0).astype(jnp.int32)
    starts = [
        (2 * (outer ^ turn) + (inner ^ chunk)) * rows for turn in range(count) for chunk in range(2)
    ]
    table = jnp.stack([outer, side, inner, encoder] + starts).astype(jnp.int32)

    def moved(value, swap_seq, swap_mp):
        pairs = [
            (s * mp + m, (s ^ swap_seq) * mp + (m ^ swap_mp)) for s in range(seq) for m in range(mp)
        ]
        return lax.ppermute(value, ("seq", "mp"), pairs)

    def handed(value, swap_seq, swap_mp):
        pairs = [
            (s * mp + m, seq * mp + (s ^ swap_seq) * mp + (m ^ swap_mp)) for s in range(seq) for m in range(mp)
        ]
        return lax.ppermute(value, ("segment", "seq", "mp"), pairs)

    def turned(value, turn):
        return lax.ppermute(value, "seq", [(s, s ^ (2 * turn)) for s in range(seq)]) if turn else value

    def chosen(array, index):
        return lax.dynamic_index_in_dim(array, index, 0, keepdims=False)

    source_here = handed(memory[0], 0, 0)
    hidden_own = chosen(hidden[0], inner)
    query_beside = moved(hidden_own, 0, 1)
    memory_own = chosen(memory[0], inner)
    source_beside = handed(memory_own, 0, 1)
    hidden_later, memory_later, _, _ = lax.optimization_barrier((hidden[0], memory[0], hidden_own, memory_own))
    hidden_away = chosen(hidden_later, 1 - inner)
    query_across = moved(hidden_away, 1, 0)
    memory_away = chosen(memory_later, 1 - inner)
    source_across = handed(memory_away, 1, 0)

    gains = (in_hbm(norm_gain), in_hbm(final_gain.reshape(1, -1)))
    weights = (w_key, w_value, w_query)
    shares = begin(table, hidden_own, source_here, gains, weights)
    hidden_away, memory_away, shares = lax.optimization_barrier((hidden_away, memory_away, shares))
    query_corner = moved(hidden_away, 1, 1)
    source_corner = handed(memory_away, 1, 1)

    turns = range(count - 1, -1, -1)
    products = end(table, query_beside, source_beside, gains, weights, shares, count)
    first = {t: turned(products[t], t) for t in turns}
    second = project(table, query_across, query_corner, source_across, source_corner, gains, weights, count)
    first_queries, second = lax.optimization_barrier((products[count:], second))
    second = {t: turned(second[t], t) for t in turns}
    first_queries = {t: turned(first_queries[t], t) for t in turns}
    keyed = [part[t] for t in range(count) for part in (first, second)]

    lengths = lengths.reshape(-1)
    context = attend(table, lengths, [(second[t], 2) for t in range(count)], keyed, 1, width)
    context = [turned(context[t], t) for t in range(count)]
    corner, across = output_parts(table, context, w_out[0])
    corner = moved(corner, 1, 1)
    across = moved(across, 1, 0)

    context = attend(table, lengths, [(first_queries[t], 0) for t in range(count)], keyed, 0, width)
    context = [turned(context[t], t) for t in range(count)]
    beside, own = output_parts(table, context, w_out[0])
    beside = moved(beside, 0, 1)
    return add_all(table, hidden, own, beside, across, corner)


def solution(mesh):
    seq, mp = mesh.shape["seq"], mesh.shape["mp"]

    def chosen(*arrays):
        batch, columns = arrays[0].shape[1], arrays[2].shape[2]
        count = seq // 2
        fits = (
            batch == 2
            and mp == 2
            and seq % 2 == 0
            and count & (count - 1) == 0
            and (columns // mp) % (count * LANES) == 0
            and (arrays[0].shape[2] // seq) % 16 == 0
        )
        return jax.shard_map(
            body if fits else gathered_body,
            mesh=mesh,
            in_specs=(
                P("segment", None, "seq", "mp"),
                P("segment", None, "seq", "mp"),
                P("segment", None, "mp"),
                P("segment", None, "mp"),
                P("segment", None, "mp"),
                P("segment", "mp", None),
                P("segment", None),
                P(),
                P("segment", None, None),
            ),
            out_specs=P("segment", None, "seq", "mp"),
            check_vma=False,
        )(*arrays)

    return chosen
```

```python
import functools

import jax
import jax.numpy as jnp
from jax import lax
from jax.experimental import pallas as pl
from jax.experimental.pallas import tpu as pltpu
from jax.sharding import PartitionSpec as P

DH = 64
LANES = 128
SCALE = 0.25 * 1.4426950408889634
MIB = 1024 * 1024
SMALL = pl.CostEstimate(flops=1, bytes_accessed=1, transcendentals=0)
IN_VMEM = pl.BlockSpec(memory_space=pltpu.VMEM)


def passed_along(value, axis, steps):
    count = lax.axis_size(axis)
    leading, last = (max(0, -steps), min(count, count - steps))
    return lax.ppermute(value, axis, [(source, source + steps) for source in range(leading, last)])


def normalize(values, gain_row):
    widened = values.astype(jnp.float32)
    square = jnp.mean(widened * widened, axis=-1, keepdims=True)
    return (widened * lax.rsqrt(square + 1e-06) * gain_row).astype(jnp.bfloat16)


def gathered_body(hidden, memory, w_query, w_key, w_value, w_out, norm_gain, final_gain, lengths):
    encoder_side = lax.axis_index("segment") == 0
    own_part = hidden[0]
    arrived = passed_along(memory[0], "segment", 1)
    source_part = jnp.where(encoder_side, own_part, arrived)
    query_rows, source_rows = (
        lax.all_gather(own_part, "mp", axis=2, tiled=True),
        lax.all_gather(source_part, "mp", axis=2, tiled=True),
    )
    batch = own_part.shape[0]
    row_count = own_part.shape[1]
    width = query_rows.shape[2]
    key_gain = jnp.where(encoder_side, norm_gain[0], final_gain)
    query_in = normalize(query_rows.reshape(batch * row_count, width), norm_gain[0])
    key_in = normalize(source_rows.reshape(batch * row_count, width), key_gain)
    head_cols = w_query.shape[2]
    local_heads = head_cols // DH
    queries = jnp.dot(query_in, w_query[0], preferred_element_type=jnp.float32).astype(jnp.bfloat16)
    keys = jnp.dot(key_in, w_key[0], preferred_element_type=jnp.float32).astype(jnp.bfloat16)
    values = jnp.dot(key_in, w_value[0], preferred_element_type=jnp.float32).astype(jnp.bfloat16)
    keys = keys.reshape(batch, row_count, head_cols)
    values = values.reshape(batch, row_count, head_cols)
    query_length = lengths[0, :, 0]
    key_length = lengths[0, :, 1]
    split_queries = queries.reshape(batch, row_count, local_heads, DH)
    key_piece = lax.all_gather(keys, "seq", axis=1, tiled=True)
    value_piece = lax.all_gather(values, "seq", axis=1, tiled=True)
    key_count = key_piece.shape[1]
    scores = (
        jnp.einsum(
            "bqhd,bkhd->bqhk",
            split_queries,
            key_piece.reshape(batch, key_count, local_heads, DH),
            preferred_element_type=jnp.float32,
        )
        * 0.25
    )
    visible = jnp.arange(key_count)[None, :] < key_length[:, None]
    mask = visible[:, None, None, :]
    scores = jnp.where(mask, scores, -1e30)
    largest = jnp.max(scores, axis=-1)
    exponent = jnp.where(mask, jnp.exp(scores - largest[..., None]), 0.0)
    totals = jnp.sum(exponent, axis=-1)
    weighted = jnp.einsum(
        "bqhk,bkhd->bqhd",
        exponent.astype(jnp.bfloat16),
        value_piece.reshape(batch, key_count, local_heads, DH),
        preferred_element_type=jnp.float32,
    )
    context = weighted / totals[..., None]
    positions = lax.axis_index("seq") * row_count + jnp.arange(row_count)
    live_rows = positions[None, :] < query_length[:, None]
    context = jnp.where(live_rows[:, :, None, None], context, 0.0)
    context = context.astype(jnp.bfloat16).reshape(batch * row_count, head_cols)
    partial_value = jnp.dot(context, w_out[0], preferred_element_type=jnp.float32)
    branch = lax.psum_scatter(
        partial_value.astype(jnp.bfloat16), "mp", scatter_dimension=1, tiled=True
    ).astype(jnp.float32)
    branch = branch.reshape(batch, row_count, branch.shape[1])
    return (own_part.astype(jnp.float32) + branch).astype(jnp.bfloat16)[None]


HEAD, SIDE, INNER, ENC = 0, 1, 2, 3
BLOCK = 4


def in_hbm(array):
    return pltpu.with_memory_space_constraint(array, pltpu.HBM)


def split_kernel(table, hidden, memory, hidden_own, memory_own, hidden_away, memory_away, sems):
    inner = table[INNER]
    copies = [
        pltpu.make_async_copy(hidden.at[0, inner], hidden_own, sems.at[0]),
        pltpu.make_async_copy(memory.at[0, inner], memory_own, sems.at[1]),
        pltpu.make_async_copy(hidden.at[0, 1 - inner], hidden_away, sems.at[2]),
        pltpu.make_async_copy(memory.at[0, 1 - inner], memory_away, sems.at[3]),
    ]
    for copy in copies:
        copy.start()
    for copy in copies:
        copy.wait()


def split(table, hidden, memory):
    return pl.pallas_call(
        split_kernel,
        out_shape=[jax.ShapeDtypeStruct(hidden.shape[2:], jnp.bfloat16)] * 4,
        in_specs=[pl.BlockSpec(memory_space=pltpu.SMEM)] + [pl.BlockSpec(memory_space=pltpu.HBM)] * 2,
        out_specs=[pl.BlockSpec(memory_space=pltpu.VMEM)] * 4,
        scratch_shapes=[pltpu.SemaphoreType.DMA((4,))],
        compiler_params=pltpu.CompilerParams(vmem_limit_bytes=4 * MIB),
        cost_estimate=SMALL,
    )(table, in_hbm(hidden), in_hbm(memory))


def times_gain(values, gains, side, into):
    half = values.shape[1]
    wide = values.astype(jnp.float32)
    into[...] = (wide * gains[:, pl.ds(pl.multiple_of(side * half, half), half)]).astype(jnp.bfloat16)
    return jnp.sum(wide * wide, axis=-1, keepdims=True)


def start_weights(weights, halves, held, sems, parts):
    half = held.shape[2]
    size = half // parts
    copies = [[] for _ in weights]
    for n, weight in enumerate(weights):
        for h, side in enumerate(halves):
            for m in range(parts):
                source = pl.ds(pl.multiple_of(side * half + m * size, size), size)
                copy = pltpu.make_async_copy(
                    weight.at[0, source], held.at[n, h, pl.ds(m * size, size)], sems.at[n, h, m]
                )
                copy.start()
                copies[n].append(copy)
    return copies


def row_factor(total, features):
    return lax.rsqrt(total / features + 1e-06)


def fetch_kernel(parts, *refs):
    half = len(refs) // 2
    ins, outs, sems = refs[:half], refs[half:-1], refs[-1]
    copies = []
    for n, (source, target) in enumerate(zip(ins, outs)):
        size = target.shape[0] // parts
        for m in range(parts):
            rows = pl.ds(m * size, size)
            copies.append(pltpu.make_async_copy(source.at[0, rows], target.at[rows], sems.at[n, m]))
            copies[-1].start()
    for copy in copies:
        copy.wait()


def fetch(weights, parts=4):
    shape = weights[0].shape[1:]
    return pl.pallas_call(
        functools.partial(fetch_kernel, parts),
        out_shape=[pltpu.VMEM(shape, jnp.bfloat16)] * len(weights),
        in_specs=[pl.BlockSpec(memory_space=pltpu.HBM)] * len(weights),
        out_specs=[IN_VMEM] * len(weights),
        scratch_shapes=[pltpu.SemaphoreType.DMA((len(weights), parts))],
        compiler_params=pltpu.CompilerParams(vmem_limit_bytes=2 * MIB),
        cost_estimate=SMALL,
    )(*[in_hbm(w) for w in weights])


def first_kernel(count, table, qo, qn, ko, kn, gain, last_gain, wk, wv, wq, *rest):
    outs, (xk, xq, fk, fq) = rest[:count], rest[count:]
    side = table[SIDE]
    rows, half = qo.shape
    width = outs[0].shape[1] // 3

    def fill(own, other, gains, x, f):
        total = times_gain(own, gains, side, x.at[0]) + times_gain(other, gains, 1 - side, x.at[1])
        f[...] = jnp.broadcast_to(row_factor(total, 2 * half), f.shape)

    fill(qo[...], qn[...], gain, xq, fq)

    @pl.when(table[ENC] == 1)
    def _():
        xk[...] = xq[...]
        fk[...] = fq[...]

    @pl.when(table[ENC] == 0)
    def _():
        fill(ko[table[INNER]], kn[...], last_gain, xk, fk)

    def part(s):
        return pl.ds(pl.multiple_of(s * half, half), half)

    for turn in range(count - 1, -1, -1):
        columns = pl.ds(pl.multiple_of((table[HEAD] ^ turn) * width, width), width)
        for n, (x, f, w) in enumerate(((xk, fk, wk), (xk, fk, wv), (xq, fq, wq))):
            total = jnp.dot(x[0], w[part(side), columns], preferred_element_type=jnp.float32)
            total += jnp.dot(x[1], w[part(1 - side), columns], preferred_element_type=jnp.float32)
            scale = f[:, :1] * SCALE if n == 2 else f[:, :1]
            outs[turn][:, n * width : (n + 1) * width] = (total * scale).astype(jnp.bfloat16)


def project_first(table, qo, qn, ko, kn, gains, weights, count):
    rows, half = qo.shape
    width = 3 * weights[0].shape[1] // count
    return pl.pallas_call(
        functools.partial(first_kernel, count),
        out_shape=[jax.ShapeDtypeStruct((rows, width), jnp.bfloat16)] * count,
        grid_spec=pltpu.PrefetchScalarGridSpec(
            num_scalar_prefetch=1,
            grid=(1,),
            in_specs=[IN_VMEM] * (6 + len(weights)),
            out_specs=[IN_VMEM] * count,
            scratch_shapes=[pltpu.VMEM((2, rows, half), jnp.bfloat16)] * 2
            + [pltpu.VMEM((rows, LANES), jnp.float32)] * 2,
        ),
        compiler_params=pltpu.CompilerParams(vmem_limit_bytes=8 * MIB),
        cost_estimate=SMALL,
    )(table, qo, qn, ko, kn, *gains, *weights)


def project_kernel(parts, count, table, qo, qn, ko, kn, gain, last_gain, wk, wv, wq, *rest):
    outs, (xk, xq, fk, fq, held, sems) = rest[:-6], rest[-6:]
    side = table[SIDE]
    rows, half = qo.shape
    width = held.shape[3] // count
    copies = start_weights((wk, wv, wq), (side, 1 - side), held, sems, parts)

    def fill(own, other, gains, x, f):
        total = times_gain(own, gains, side, x.at[0]) + times_gain(other, gains, 1 - side, x.at[1])
        f[...] = jnp.broadcast_to(row_factor(total, 2 * half), (rows, LANES))

    fill(qo[...], qn[...], gain, xq, fq)

    @pl.when(table[ENC] == 1)
    def _():
        xk[...] = xq[...]
        fk[...] = fq[...]

    @pl.when(table[ENC] == 0)
    def _():
        fill(ko[...], kn[...], last_gain, xk, fk)

    for n, (x, f) in enumerate(((xk, fk), (xk, fk), (xq, fq))):
        for copy in copies[n]:
            copy.wait()
        scale = f[:, :1] * SCALE if n == 2 else f[:, :1]
        for turn in range(count):
            columns = pl.ds(pl.multiple_of((table[HEAD] ^ turn) * width, width), width)
            total = jnp.dot(x[0], held[n, 0, :, columns], preferred_element_type=jnp.float32)
            total += jnp.dot(x[1], held[n, 1, :, columns], preferred_element_type=jnp.float32)
            total = (total * scale).astype(jnp.bfloat16)
            outs[turn][:, n * width : (n + 1) * width] = total


def project(table, qo, qn, ko, kn, gains, weights, count, parts=4):
    rows, half = qo.shape
    columns = weights[0].shape[2]
    width = columns // count
    return pl.pallas_call(
        functools.partial(project_kernel, parts, count),
        out_shape=[jax.ShapeDtypeStruct((rows, 3 * width), jnp.bfloat16)] * count,
        grid_spec=pltpu.PrefetchScalarGridSpec(
            num_scalar_prefetch=1,
            grid=(1,),
            in_specs=[IN_VMEM] * 6 + [pl.BlockSpec(memory_space=pltpu.HBM)] * 3,
            out_specs=[IN_VMEM] * count,
            scratch_shapes=[pltpu.VMEM((2, rows, half), jnp.bfloat16)] * 2
            + [pltpu.VMEM((rows, LANES), jnp.float32)] * 2
            + [pltpu.VMEM((3, 2, half, columns), jnp.bfloat16), pltpu.SemaphoreType.DMA((3, 2, parts))],
        ),
        compiler_params=pltpu.CompilerParams(vmem_limit_bytes=32 * MIB),
        cost_estimate=SMALL,
    )(table, qo, qn, ko, kn, *gains, *[in_hbm(w) for w in weights])


def attend_kernel(count, chunk, tile, places, table, lengths, *refs):
    q_refs, keyed = refs[:count], refs[count : 3 * count]
    outs, (qs, ks, vs, contexts) = refs[3 * count : 4 * count], refs[4 * count :]
    rows, width = outs[0].shape
    pairs = width // LANES
    query_length = lengths[2 * table[INNER]]
    key_length = lengths[2 * table[INNER] + 1]
    lane = lax.broadcasted_iota(jnp.int32, (rows, LANES), 1)
    row = lax.broadcasted_iota(jnp.int32, (rows, LANES), 0)
    low = lane < DH
    zero = jnp.zeros((rows, LANES), jnp.bfloat16)
    one = jnp.ones((rows, LANES), jnp.bfloat16)
    unit = jnp.where(lane == 0, one, zero)
    for j in range(2 * count):
        here = pl.ds(j * rows, rows)
        hides = jnp.logical_and(lane == 0, row + table[BLOCK + j] >= key_length)
        bias = jnp.where(hides, -1e30, 0.0).astype(jnp.bfloat16)
        for pair in range(pairs):
            columns = slice(pair * LANES, (pair + 1) * LANES)
            key = keyed[j][:, columns]
            value = keyed[j][:, width + pair * LANES : width + (pair + 1) * LANES]
            ks[pair, 0, here, :LANES] = jnp.where(low, key, zero)
            ks[pair, 1, here, :LANES] = jnp.where(low, zero, key)
            ks[pair, 0, here, LANES:] = bias
            ks[pair, 1, here, LANES:] = bias
            vs[pair, 0, here, :] = jnp.where(low, value, one)
            vs[pair, 1, here, :] = jnp.where(low, one, value)
    for j in range(count):
        here = pl.ds(j * rows, rows)
        for pair in range(pairs):
            start = places[j] * width + pair * LANES
            qs[pair, here, :LANES] = q_refs[j][:, start : start + LANES]
            qs[pair, here, LANES:] = unit

    low = lax.broadcasted_iota(jnp.int32, (tile, LANES), 1) < DH
    for pair in range(pairs):
        for t in range(count * rows // tile):
            query = qs[pair, pl.ds(t * tile, tile), :]
            sums = []
            for head in range(2):
                scores = lax.dot_general(
                    query, ks[pair, head], (((1,), (1,)), ((), ())), preferred_element_type=jnp.float32
                )
                largest = jnp.max(scores, axis=-1, keepdims=True)
                weights = jnp.exp2(scores - largest).astype(jnp.bfloat16)
                sums.append(jnp.dot(weights, vs[pair, head], preferred_element_type=jnp.float32))
            weighted = jnp.where(low, sums[0], sums[1])
            totals = jnp.where(low, pltpu.roll(sums[0], DH, 1), pltpu.roll(sums[1], DH, 1))
            contexts[pl.ds(t * tile, tile), pair * LANES : (pair + 1) * LANES] = (weighted / totals).astype(
                jnp.bfloat16
            )

    for j in range(count):
        live = row + table[BLOCK + 2 * j + chunk] < query_length
        for pair in range(pairs):
            columns = slice(pair * LANES, (pair + 1) * LANES)
            outs[j][:, columns] = jnp.where(live, contexts[pl.ds(j * rows, rows), columns], zero)


def attend(table, lengths, queries, keyed, chunk, width):
    count = len(queries)
    rows = queries[0][0].shape[0]
    total = 2 * count * rows

    return pl.pallas_call(
        functools.partial(
            attend_kernel, count, chunk, 2 * rows if count % 2 == 0 else rows, [place for _, place in queries]
        ),
        out_shape=[jax.ShapeDtypeStruct((rows, width), jnp.bfloat16)] * count,
        grid_spec=pltpu.PrefetchScalarGridSpec(
            num_scalar_prefetch=2,
            grid=(1,),
            in_specs=[IN_VMEM] * (3 * count),
            out_specs=[IN_VMEM] * count,
            scratch_shapes=[
                pltpu.VMEM((width // LANES, count * rows, 2 * LANES), jnp.bfloat16),
                pltpu.VMEM((width // LANES, 2, total, 2 * LANES), jnp.bfloat16),
                pltpu.VMEM((width // LANES, 2, total, LANES), jnp.bfloat16),
                pltpu.VMEM((count * rows, width), jnp.bfloat16),
            ],
        ),
        compiler_params=pltpu.CompilerParams(vmem_limit_bytes=32 * MIB),
        cost_estimate=SMALL,
    )(table, lengths, *[array for array, _ in queries], *keyed)


def output_kernel(count, table, w, *refs):
    pieces, outs, x = refs[:count], refs[count : count + 2], refs[-1]
    width = pieces[0].shape[1]
    half = outs[0].shape[1]
    for turn in range(count):
        place = pl.multiple_of((table[HEAD] ^ turn) * width, width)
        x[:, pl.ds(place, width)] = pieces[turn][...]
    for i in range(2):
        columns = pl.ds(pl.multiple_of((1 - (table[SIDE] ^ i)) * half, half), half)
        outs[i][...] = jnp.dot(x[...], w[:, columns], preferred_element_type=jnp.float32).astype(jnp.bfloat16)


def output_parts(table, pieces, w_out):
    rows, width = pieces[0].shape
    depth, half = w_out.shape[0], w_out.shape[1] // 2
    return pl.pallas_call(
        functools.partial(output_kernel, len(pieces)),
        out_shape=[jax.ShapeDtypeStruct((rows, half), jnp.bfloat16)] * 2,
        grid_spec=pltpu.PrefetchScalarGridSpec(
            num_scalar_prefetch=1,
            grid=(1,),
            in_specs=[IN_VMEM] * (1 + len(pieces)),
            out_specs=[IN_VMEM] * 2,
            scratch_shapes=[pltpu.VMEM((rows, depth), jnp.bfloat16)],
        ),
        compiler_params=pltpu.CompilerParams(vmem_limit_bytes=16 * MIB),
        cost_estimate=SMALL,
    )(table, w_out, *pieces)


def add_kernel(table, hidden, own, beside, across, corner, out):
    def total(a, b):
        out[0, 0] = (
            hidden[0, 0].astype(jnp.float32) + (a[...].astype(jnp.float32) + b[...].astype(jnp.float32))
        ).astype(jnp.bfloat16)

    @pl.when(pl.program_id(0) == 0)
    def _():
        total(own, beside)

    @pl.when(pl.program_id(0) == 1)
    def _():
        total(across, corner)


def add_all(table, hidden, own, beside, across, corner):
    rows, half = own.shape
    block = pl.BlockSpec((1, 1, rows, half), lambda i, table: (0, table[INNER] ^ i, 0, 0))
    part = pl.BlockSpec((rows, half), lambda i, table: (0, 0))
    return pl.pallas_call(
        add_kernel,
        out_shape=jax.ShapeDtypeStruct(hidden.shape, jnp.bfloat16),
        grid_spec=pltpu.PrefetchScalarGridSpec(
            num_scalar_prefetch=1,
            grid=(2,),
            in_specs=[block, part, part, part, part],
            out_specs=block,
        ),
        compiler_params=pltpu.CompilerParams(vmem_limit_bytes=16 * MIB),
    )(table, hidden, own, beside, across, corner)


def body(hidden, memory, w_query, w_key, w_value, w_out, norm_gain, final_gain, lengths):
    seq, mp = lax.axis_size("seq"), lax.axis_size("mp")
    count = seq // 2
    rows, half = hidden.shape[2:]
    width = w_query.shape[2] // count

    place, side = lax.axis_index("seq"), lax.axis_index("mp")
    outer, inner = place // 2, place % 2
    encoder = (lax.axis_index("segment") == 0).astype(jnp.int32)
    starts = [
        (2 * (outer ^ turn) + (inner ^ chunk)) * rows for turn in range(count) for chunk in range(2)
    ]
    table = jnp.stack([outer, side, inner, encoder] + starts).astype(jnp.int32)

    def moved(value, swap_seq, swap_mp, segments=(0, 1)):
        pairs = [
            ((g * seq + s) * mp + m, (g * seq + (s ^ swap_seq)) * mp + (m ^ swap_mp))
            for g in segments
            for s in range(seq)
            for m in range(mp)
        ]
        return lax.ppermute(value, ("segment", "seq", "mp"), pairs)

    def handed(value, swap_seq, swap_mp):
        pairs = [
            (s * mp + m, seq * mp + (s ^ swap_seq) * mp + (m ^ swap_mp)) for s in range(seq) for m in range(mp)
        ]
        return lax.ppermute(value, ("segment", "seq", "mp"), pairs)

    def turned(value, turn):
        return moved(value, 2 * turn, 0) if turn else value

    def after(value, *others):
        return lax.optimization_barrier((value, *others))[0]

    hidden_own, memory_own, hidden_away, memory_away = split(table, hidden, memory)
    query_beside = moved(hidden_own, 0, 1)
    source_beside = handed(memory_own, 0, 1)
    source_here = handed(after(memory[0], hidden_own), 0, 0)
    query_across = moved(hidden_away, 1, 0)
    source_across = handed(memory_away, 1, 0)
    weights = (w_key, w_value, w_query)
    fetched = fetch([after(w, query_beside) for w in weights])

    gains = (in_hbm(norm_gain), in_hbm(final_gain.reshape(1, -1)))
    turns = range(count - 1, -1, -1)
    products = project_first(table, hidden_own, query_beside, source_here, source_beside, gains, fetched, count)
    first = {t: turned(products[t], t) for t in turns}
    query_corner = moved(after(query_across, fetched), 0, 1)
    source_corner = moved(after(source_across, fetched), 0, 1, (1,))
    query_across = after(query_across, products)
    products = project(table, query_across, query_corner, source_across, source_corner, gains, weights, count)
    second = {t: turned(after(products[t], first[1]) if t == 1 else products[t], t) for t in turns}
    keyed = [part[t] for t in range(count) for part in (first, second)]

    lengths = lengths.reshape(-1)
    context = attend(table, lengths, [(second[t], 2) for t in range(count)], keyed, 1, width)
    second_context = [moved(context[t], 2 * t + 1, 0) for t in range(count)]
    queries = [(after(first[t], context), 2) for t in range(count)]
    context = attend(table, lengths, queries, keyed, 0, width)
    first_context = [moved(after(context[t], second_context), 2 * t, 0) if t else context[t] for t in range(count)]
    away, second_own = output_parts(table, second_context, w_out[0])
    second_beside = moved(away, 0, 1)
    away, own = output_parts(table, first_context, w_out[0])
    first_beside = moved(away, 0, 1)
    return add_all(table, hidden, own, first_beside, second_own, second_beside)


def solution(mesh):
    seq, mp = mesh.shape["seq"], mesh.shape["mp"]

    def chosen(*arrays):
        batch, columns = arrays[0].shape[1], arrays[2].shape[2]
        count = seq // 2
        fits = (
            batch == 2
            and mp == 2
            and seq % 2 == 0
            and count & (count - 1) == 0
            and (columns // mp) % (count * LANES) == 0
            and (arrays[0].shape[2] // seq) % 16 == 0
        )
        return jax.shard_map(
            body if fits else gathered_body,
            mesh=mesh,
            in_specs=(
                P("segment", None, "seq", "mp"),
                P("segment", None, "seq", "mp"),
                P("segment", None, "mp"),
                P("segment", None, "mp"),
                P("segment", None, "mp"),
                P("segment", "mp", None),
                P("segment", None),
                P(),
                P("segment", None, None),
            ),
            out_specs=P("segment", None, "seq", "mp"),
            check_vma=False,
        )(*arrays)

    return chosen
```

```python
import functools

import jax
import jax.numpy as jnp
from jax import lax
from jax.experimental import pallas as pl
from jax.experimental.pallas import tpu as pltpu
from jax.sharding import PartitionSpec as P

DH = 64
LANES = 128
SCALE = 0.25 * 1.4426950408889634
MIB = 1024 * 1024
SMALL = pl.CostEstimate(flops=1, bytes_accessed=1, transcendentals=0)
IN_VMEM = pl.BlockSpec(memory_space=pltpu.VMEM)


def passed_along(value, axis, steps):
    count = lax.axis_size(axis)
    leading, last = (max(0, -steps), min(count, count - steps))
    return lax.ppermute(value, axis, [(source, source + steps) for source in range(leading, last)])


def normalize(values, gain_row):
    widened = values.astype(jnp.float32)
    square = jnp.mean(widened * widened, axis=-1, keepdims=True)
    return (widened * lax.rsqrt(square + 1e-06) * gain_row).astype(jnp.bfloat16)


def gathered_body(hidden, memory, w_query, w_key, w_value, w_out, norm_gain, final_gain, lengths):
    encoder_side = lax.axis_index("segment") == 0
    own_part = hidden[0]
    arrived = passed_along(memory[0], "segment", 1)
    source_part = jnp.where(encoder_side, own_part, arrived)
    query_rows, source_rows = (
        lax.all_gather(own_part, "mp", axis=2, tiled=True),
        lax.all_gather(source_part, "mp", axis=2, tiled=True),
    )
    batch = own_part.shape[0]
    row_count = own_part.shape[1]
    width = query_rows.shape[2]
    key_gain = jnp.where(encoder_side, norm_gain[0], final_gain)
    query_in = normalize(query_rows.reshape(batch * row_count, width), norm_gain[0])
    key_in = normalize(source_rows.reshape(batch * row_count, width), key_gain)
    head_cols = w_query.shape[2]
    local_heads = head_cols // DH
    queries = jnp.dot(query_in, w_query[0], preferred_element_type=jnp.float32).astype(jnp.bfloat16)
    keys = jnp.dot(key_in, w_key[0], preferred_element_type=jnp.float32).astype(jnp.bfloat16)
    values = jnp.dot(key_in, w_value[0], preferred_element_type=jnp.float32).astype(jnp.bfloat16)
    keys = keys.reshape(batch, row_count, head_cols)
    values = values.reshape(batch, row_count, head_cols)
    query_length = lengths[0, :, 0]
    key_length = lengths[0, :, 1]
    split_queries = queries.reshape(batch, row_count, local_heads, DH)
    key_piece = lax.all_gather(keys, "seq", axis=1, tiled=True)
    value_piece = lax.all_gather(values, "seq", axis=1, tiled=True)
    key_count = key_piece.shape[1]
    scores = (
        jnp.einsum(
            "bqhd,bkhd->bqhk",
            split_queries,
            key_piece.reshape(batch, key_count, local_heads, DH),
            preferred_element_type=jnp.float32,
        )
        * 0.25
    )
    visible = jnp.arange(key_count)[None, :] < key_length[:, None]
    mask = visible[:, None, None, :]
    scores = jnp.where(mask, scores, -1e30)
    largest = jnp.max(scores, axis=-1)
    exponent = jnp.where(mask, jnp.exp(scores - largest[..., None]), 0.0)
    totals = jnp.sum(exponent, axis=-1)
    weighted = jnp.einsum(
        "bqhk,bkhd->bqhd",
        exponent.astype(jnp.bfloat16),
        value_piece.reshape(batch, key_count, local_heads, DH),
        preferred_element_type=jnp.float32,
    )
    context = weighted / totals[..., None]
    positions = lax.axis_index("seq") * row_count + jnp.arange(row_count)
    live_rows = positions[None, :] < query_length[:, None]
    context = jnp.where(live_rows[:, :, None, None], context, 0.0)
    context = context.astype(jnp.bfloat16).reshape(batch * row_count, head_cols)
    partial_value = jnp.dot(context, w_out[0], preferred_element_type=jnp.float32)
    branch = lax.psum_scatter(
        partial_value.astype(jnp.bfloat16), "mp", scatter_dimension=1, tiled=True
    ).astype(jnp.float32)
    branch = branch.reshape(batch, row_count, branch.shape[1])
    return (own_part.astype(jnp.float32) + branch).astype(jnp.bfloat16)[None]


HEAD, SIDE, INNER, ENC = 0, 1, 2, 3
BLOCK = 4


def in_hbm(array):
    return pltpu.with_memory_space_constraint(array, pltpu.HBM)


def split_kernel(table, hidden, memory, own, away, sems):
    inner = table[INNER]

    def copied(array):
        copies = [
            pltpu.make_async_copy(array.at[0, inner], own, sems.at[0]),
            pltpu.make_async_copy(array.at[0, 1 - inner], away, sems.at[1]),
        ]
        for copy in copies:
            copy.start()
        for copy in copies:
            copy.wait()

    if memory is None:
        copied(hidden)
    else:
        pl.when(table[ENC] == 1)(lambda: copied(hidden))
        pl.when(table[ENC] == 0)(lambda: copied(memory))


def split(table, hidden, memory=None):
    arrays = [hidden] if memory is None else [hidden, memory]

    def kernel(table, hidden, *rest):
        split_kernel(table, hidden, *([None] if memory is None else []), *rest)

    return pl.pallas_call(
        kernel,
        out_shape=[jax.ShapeDtypeStruct(hidden.shape[2:], jnp.bfloat16)] * 2,
        in_specs=[pl.BlockSpec(memory_space=pltpu.SMEM)] + [pl.BlockSpec(memory_space=pltpu.HBM)] * len(arrays),
        out_specs=[IN_VMEM] * 2,
        scratch_shapes=[pltpu.SemaphoreType.DMA((2,))],
        compiler_params=pltpu.CompilerParams(vmem_limit_bytes=4 * MIB),
        cost_estimate=SMALL,
    )(table, *[in_hbm(array) for array in arrays])


def mark(array):
    def kernel(array, out):
        out[...] = jnp.zeros(out.shape, out.dtype)

    return pl.pallas_call(
        kernel,
        out_shape=jax.ShapeDtypeStruct((8, LANES), jnp.float32),
        in_specs=[pl.BlockSpec(memory_space=pl.ANY)],
        out_specs=IN_VMEM,
        compiler_params=pltpu.CompilerParams(vmem_limit_bytes=MIB),
        cost_estimate=pl.CostEstimate(flops=0, bytes_accessed=8 * MIB, transcendentals=0),
    )(array)


def times_gain(values, gains, side, into):
    half = values.shape[1]
    wide = values.astype(jnp.float32)
    into[...] = (wide * gains[:, pl.ds(pl.multiple_of(side * half, half), half)]).astype(jnp.bfloat16)
    return jnp.sum(wide * wide, axis=-1, keepdims=True)


def row_factor(total, features):
    return lax.rsqrt(total / features + 1e-06)


def project_kernel(parts, count, queried, table, *refs):
    size = 4 if queried else 2
    rest = refs[size:]
    (gain, last_gain), weights, rest = rest[:2], rest[2 : 2 + size // 2 + 1], rest[2 + size // 2 + 1 :]
    outs, (xk, xq, fk, fq, held, sems) = rest[:count], rest[count:]
    side = table[SIDE]
    rows, half = refs[0].shape
    width = held.shape[2] // count
    copies = []
    piece = 2 * half // parts
    for n, weight in enumerate(weights):
        for m in range(parts):
            here = pl.ds(m * piece, piece)
            copies.append(pltpu.make_async_copy(weight.at[0, here], held.at[n, here], sems.at[n, m]))
    ahead = len(copies)
    for copy in copies[:ahead]:
        copy.start()

    def fill(own, other, gains, x, f):
        total = times_gain(own, gains, side, x.at[0]) + times_gain(other, gains, 1 - side, x.at[1])
        f[...] = jnp.broadcast_to(row_factor(total, 2 * half), (rows, LANES))

    if queried:
        qo, qn, ko, kn = refs[:4]
        fill(qo[...], qn[...], gain, xq, fq)

        @pl.when(table[ENC] == 1)
        def _():
            xk[...] = xq[...]
            fk[...] = fq[...]

    else:
        ko, kn = refs[:2]

        @pl.when(table[ENC] == 1)
        def _():
            fill(ko[...], kn[...], gain, xk, fk)

    @pl.when(table[ENC] == 0)
    def _():
        fill(ko[...], kn[...], last_gain, xk, fk)

    def part(s):
        return pl.ds(pl.multiple_of(s * half, half), half)

    for n in range(len(weights)):
        for m in range(n * parts, (n + 1) * parts):
            copies[m].wait()
            if m + ahead < len(copies):
                copies[m + ahead].start()
        x, f = (xq, fq) if n == 2 else (xk, fk)
        scale = f[:, :1] * SCALE if n == 2 else f[:, :1]
        for turn in range(count - 1, -1, -1):
            columns = pl.ds(pl.multiple_of((table[HEAD] ^ turn) * width, width), width)
            total = jnp.dot(x[0], held[n, part(side), columns], preferred_element_type=jnp.float32)
            total += jnp.dot(x[1], held[n, part(1 - side), columns], preferred_element_type=jnp.float32)
            outs[turn][:, n * width : (n + 1) * width] = (total * scale).astype(jnp.bfloat16)


def project(table, arrays, gains, weights, count, parts=1):
    rows, half = arrays[0].shape
    columns = weights[0].shape[2]
    queried = len(arrays) == 4
    weights = weights[: 3 if queried else 2]
    width = len(weights) * columns // count
    return pl.pallas_call(
        functools.partial(project_kernel, parts, count, queried),
        out_shape=[jax.ShapeDtypeStruct((rows, width), jnp.bfloat16)] * count,
        grid_spec=pltpu.PrefetchScalarGridSpec(
            num_scalar_prefetch=1,
            grid=(1,),
            in_specs=[IN_VMEM] * (len(arrays) + 2) + [pl.BlockSpec(memory_space=pltpu.HBM)] * len(weights),
            out_specs=[IN_VMEM] * count,
            scratch_shapes=[pltpu.VMEM((2, rows, half), jnp.bfloat16)] * 2
            + [pltpu.VMEM((rows, LANES), jnp.float32)] * 2
            + [
                pltpu.VMEM((len(weights), 2 * half, columns), jnp.bfloat16),
                pltpu.SemaphoreType.DMA((len(weights), parts)),
            ],
        ),
        compiler_params=pltpu.CompilerParams(vmem_limit_bytes=24 * MIB),
        cost_estimate=SMALL,
    )(table, *arrays, *gains, *[in_hbm(w) for w in weights])


def attend_kernel(chosen, tile, blocks, table, lengths, *refs):
    arrays, outs, (qs, ks, vs, contexts) = refs[:blocks], refs[blocks:-4], refs[-4:]
    rows, width = outs[0].shape
    pairs = width // LANES
    query_length = lengths[2 * table[INNER]]
    key_length = lengths[2 * table[INNER] + 1]
    lane = lax.broadcasted_iota(jnp.int32, (rows, LANES), 1)
    row = lax.broadcasted_iota(jnp.int32, (rows, LANES), 0)
    low = lane < DH
    zero = jnp.zeros((rows, LANES), jnp.bfloat16)
    one = jnp.ones((rows, LANES), jnp.bfloat16)
    unit = jnp.where(lane == 0, one, zero)

    def lanes(block):
        return slice(block * LANES, (block + 1) * LANES)

    for j in range(blocks):
        here = pl.ds(j * rows, rows)
        hides = jnp.logical_and(lane == 0, row + table[BLOCK + j] >= key_length)
        bias = jnp.where(hides, -1e30, 0.0).astype(jnp.bfloat16)
        for pair in range(pairs):
            key = arrays[j][:, lanes(pair)]
            value = arrays[j][:, lanes(pairs + pair)]
            ks[pair, 0, here, :LANES] = jnp.where(low, key, zero)
            ks[pair, 1, here, :LANES] = jnp.where(low, zero, key)
            ks[pair, 0, here, LANES:] = bias
            ks[pair, 1, here, LANES:] = bias
            vs[pair, 0, here, :] = jnp.where(low, value, one)
            vs[pair, 1, here, :] = jnp.where(low, one, value)
    for i, j in enumerate(chosen):
        here = pl.ds(i * rows, rows)
        for pair in range(pairs):
            qs[pair, here, :LANES] = arrays[j][:, lanes(2 * pairs + pair)]
            qs[pair, here, LANES:] = unit

    low = lax.broadcasted_iota(jnp.int32, (tile, LANES), 1) < DH
    for pair in range(pairs):
        for t in range(len(chosen) * rows // tile):
            here = pl.ds(t * tile, tile)
            sums = []
            for head in range(2):
                scores = lax.dot_general(
                    qs[pair, here, :], ks[pair, head], (((1,), (1,)), ((), ())), preferred_element_type=jnp.float32
                )
                largest = jnp.max(scores, axis=-1, keepdims=True)
                weights = jnp.exp2(scores - largest).astype(jnp.bfloat16)
                sums.append(jnp.dot(weights, vs[pair, head], preferred_element_type=jnp.float32))
            weighted = jnp.where(low, sums[0], sums[1])
            totals = jnp.where(low, pltpu.roll(sums[0], DH, 1), pltpu.roll(sums[1], DH, 1))
            contexts[here, lanes(pair)] = (weighted / totals).astype(jnp.bfloat16)

    for i, j in enumerate(chosen):
        live = row + table[BLOCK + j] < query_length
        for pair in range(pairs):
            outs[i][:, lanes(pair)] = jnp.where(live, contexts[pl.ds(i * rows, rows), lanes(pair)], zero)


def attend(table, lengths, arrays, chosen, width):
    rows = arrays[0].shape[0]
    total = len(arrays) * rows
    size = len(chosen) * rows
    pairs = width // LANES
    return pl.pallas_call(
        functools.partial(attend_kernel, chosen, size, len(arrays)),
        out_shape=[jax.ShapeDtypeStruct((rows, width), jnp.bfloat16)] * len(chosen),
        grid_spec=pltpu.PrefetchScalarGridSpec(
            num_scalar_prefetch=2,
            grid=(1,),
            in_specs=[IN_VMEM] * len(arrays),
            out_specs=[IN_VMEM] * len(chosen),
            scratch_shapes=[
                pltpu.VMEM((pairs, size, 2 * LANES), jnp.bfloat16),
                pltpu.VMEM((pairs, 2, total, 2 * LANES), jnp.bfloat16),
                pltpu.VMEM((pairs, 2, total, LANES), jnp.bfloat16),
                pltpu.VMEM((size, width), jnp.bfloat16),
            ],
        ),
        compiler_params=pltpu.CompilerParams(vmem_limit_bytes=32 * MIB),
        cost_estimate=SMALL,
    )(table, lengths, *arrays)


def output_kernel(count, table, w, *refs):
    pieces, outs, x = refs[:count], refs[count : count + 2], refs[-1]
    width = pieces[0].shape[1]
    half = outs[0].shape[1]
    for turn in range(count):
        place = pl.multiple_of((table[HEAD] ^ turn) * width, width)
        x[:, pl.ds(place, width)] = pieces[turn][...]
    for i in range(2):
        columns = pl.ds(pl.multiple_of((1 - (table[SIDE] ^ i)) * half, half), half)
        outs[i][...] = jnp.dot(x[...], w[:, columns], preferred_element_type=jnp.float32).astype(jnp.bfloat16)


def output_parts(table, pieces, w_out):
    rows, width = pieces[0].shape
    depth, half = w_out.shape[0], w_out.shape[1] // 2
    return pl.pallas_call(
        functools.partial(output_kernel, len(pieces)),
        out_shape=[jax.ShapeDtypeStruct((rows, half), jnp.bfloat16)] * 2,
        grid_spec=pltpu.PrefetchScalarGridSpec(
            num_scalar_prefetch=1,
            grid=(1,),
            in_specs=[IN_VMEM] * (1 + len(pieces)),
            out_specs=[IN_VMEM] * 2,
            scratch_shapes=[pltpu.VMEM((rows, depth), jnp.bfloat16)],
        ),
        compiler_params=pltpu.CompilerParams(vmem_limit_bytes=16 * MIB),
        cost_estimate=SMALL,
    )(table, w_out, *pieces)


def add_kernel(table, hidden, own, beside, across, corner, out):
    def total(a, b):
        out[0, 0] = (
            hidden[0, 0].astype(jnp.float32) + (a[...].astype(jnp.float32) + b[...].astype(jnp.float32))
        ).astype(jnp.bfloat16)

    @pl.when(pl.program_id(0) == 0)
    def _():
        total(own, beside)

    @pl.when(pl.program_id(0) == 1)
    def _():
        total(across, corner)


def add_all(table, hidden, own, beside, across, corner):
    rows, half = own.shape
    block = pl.BlockSpec((1, 1, rows, half), lambda i, table: (0, table[INNER] ^ i, 0, 0))
    part = pl.BlockSpec((rows, half), lambda i, table: (0, 0))
    return pl.pallas_call(
        add_kernel,
        out_shape=jax.ShapeDtypeStruct(hidden.shape, jnp.bfloat16),
        grid_spec=pltpu.PrefetchScalarGridSpec(
            num_scalar_prefetch=1,
            grid=(2,),
            in_specs=[block, part, part, part, part],
            out_specs=block,
        ),
        compiler_params=pltpu.CompilerParams(vmem_limit_bytes=16 * MIB),
    )(table, hidden, own, beside, across, corner)


def body(hidden, memory, w_query, w_key, w_value, w_out, norm_gain, final_gain, lengths):
    seq, mp = lax.axis_size("seq"), lax.axis_size("mp")
    width = w_query.shape[2] // 2
    rows = hidden.shape[2]

    place, side = lax.axis_index("seq"), lax.axis_index("mp")
    encoder = (lax.axis_index("segment") == 0).astype(jnp.int32)
    chunks = range(0, seq, 2)
    starts = [(place ^ (chunk + turn)) * rows for chunk in chunks for turn in range(2)]
    table = jnp.stack([place % 2, side, place // 2 % 2, encoder] + starts).astype(jnp.int32)

    def moved(value, swap_seq, swap_mp, segments=(0, 1)):
        pairs = [
            ((g * seq + s) * mp + m, (g * seq + (s ^ swap_seq)) * mp + (m ^ swap_mp))
            for g in segments
            for s in range(seq)
            for m in range(mp)
        ]
        return lax.ppermute(value, ("segment", "seq", "mp"), pairs)

    def after(value, *others):
        return lax.optimization_barrier((value, *others))[0]

    gains = (in_hbm(norm_gain), in_hbm(final_gain.reshape(1, -1)))
    weights = (w_key, w_value, w_query)

    arrived = passed_along(memory[0], "segment", 1)
    hidden_own, hidden_away = split(table, hidden)
    query = {0: hidden_own}
    query_other = {0: moved(hidden_own, 0, 1)}
    query[2] = moved(hidden_away, 2, 0)
    source_own, source_away = split(table, hidden, after(arrived, hidden_own)[None])
    source = {0: source_own}
    source_other = {0: moved(source_own, 0, 1, (1,))}
    source[2] = moved(source_away, 2, 0, (1,))
    if seq > 4:
        source[4] = moved(source_own, 4, 0)
    query_other[2] = moved(query[2], 0, 1)
    source_other[2] = moved(source[2], 0, 1, (1,))

    def projected(chunk, *others):
        parts = [source[chunk], source_other[chunk]]
        if chunk < 4:
            parts = [query[chunk], query_other[chunk]] + parts
        parts[0] = after(parts[0], *others)
        kept, sent = project(table, parts, gains, weights, 2)
        return kept, moved(sent, 1, 0)

    done = {0: projected(0, query[2], source[2])}
    before = done[0][0]
    if seq > 4:
        source[4] = after(source[4], before)
        source_other[4] = moved(source[4], 0, 1)
        before = [before, mark(source[4])]
    last = before
    for chunk in chunks[3:]:
        source[chunk] = moved(after(source_away if chunk & 2 else source_own, last), chunk, 0)
        last = source[chunk]
    done[2] = projected(2, before)
    before = done[2][0]
    for chunk in chunks[2:]:
        if chunk > 4:
            source_other[chunk] = moved(after(source[chunk], done[2][0]), 0, 1)
        done[chunk] = projected(chunk, before, done[chunk - 4][1])
        before = done[chunk][0]
    arrays = [array for chunk in chunks for array in done[chunk]]

    lengths = lengths.reshape(-1)
    context = attend(table, lengths, arrays, (2, 3), width)
    second_context = [moved(context[turn], 2 + turn, 0) for turn in range(2)]
    context = attend(table, lengths, after(arrays, context), (0, 1), width)
    first_context = [context[0], moved(after(context[1], second_context), 1, 0)]
    away, second_own = output_parts(table, second_context, w_out[0])
    second_beside = moved(away, 0, 1)
    away, own = output_parts(table, first_context, w_out[0])
    first_beside = moved(away, 0, 1)
    return add_all(table, hidden, own, first_beside, second_own, second_beside)


def solution(mesh):
    seq, mp = mesh.shape["seq"], mesh.shape["mp"]

    def chosen(*arrays):
        batch, columns = arrays[0].shape[1], arrays[2].shape[2]
        fits = (
            batch == 2
            and mp == 2
            and seq >= 4
            and seq & (seq - 1) == 0
            and (columns // mp) % (2 * LANES) == 0
            and (arrays[0].shape[2] // seq) % 16 == 0
        )
        return jax.shard_map(
            body if fits else gathered_body,
            mesh=mesh,
            in_specs=(
                P("segment", None, "seq", "mp"),
                P("segment", None, "seq", "mp"),
                P("segment", None, "mp"),
                P("segment", None, "mp"),
                P("segment", None, "mp"),
                P("segment", "mp", None),
                P("segment", None),
                P(),
                P("segment", None, None),
            ),
            out_specs=P("segment", None, "seq", "mp"),
            check_vma=False,
        )(*arrays)

    return chosen
```

```python
import functools

import jax
import jax.numpy as jnp
from jax import lax
from jax.experimental import pallas as pl
from jax.experimental.pallas import tpu as pltpu
from jax.sharding import PartitionSpec as P

DH = 64
LANES = 128
SCALE = 0.25 * 1.4426950408889634
MIB = 1024 * 1024
SMALL = pl.CostEstimate(flops=1, bytes_accessed=1, transcendentals=0)
IN_VMEM = pl.BlockSpec(memory_space=pltpu.VMEM)


def passed_along(value, axis, steps):
    count = lax.axis_size(axis)
    leading, last = (max(0, -steps), min(count, count - steps))
    return lax.ppermute(value, axis, [(source, source + steps) for source in range(leading, last)])


def normalize(values, gain_row):
    widened = values.astype(jnp.float32)
    square = jnp.mean(widened * widened, axis=-1, keepdims=True)
    return (widened * lax.rsqrt(square + 1e-06) * gain_row).astype(jnp.bfloat16)


def gathered_body(hidden, memory, w_query, w_key, w_value, w_out, norm_gain, final_gain, lengths):
    encoder_side = lax.axis_index("segment") == 0
    own_part = hidden[0]
    arrived = passed_along(memory[0], "segment", 1)
    source_part = jnp.where(encoder_side, own_part, arrived)
    query_rows, source_rows = (
        lax.all_gather(own_part, "mp", axis=2, tiled=True),
        lax.all_gather(source_part, "mp", axis=2, tiled=True),
    )
    batch = own_part.shape[0]
    row_count = own_part.shape[1]
    width = query_rows.shape[2]
    key_gain = jnp.where(encoder_side, norm_gain[0], final_gain)
    query_in = normalize(query_rows.reshape(batch * row_count, width), norm_gain[0])
    key_in = normalize(source_rows.reshape(batch * row_count, width), key_gain)
    head_cols = w_query.shape[2]
    local_heads = head_cols // DH
    queries = jnp.dot(query_in, w_query[0], preferred_element_type=jnp.float32).astype(jnp.bfloat16)
    keys = jnp.dot(key_in, w_key[0], preferred_element_type=jnp.float32).astype(jnp.bfloat16)
    values = jnp.dot(key_in, w_value[0], preferred_element_type=jnp.float32).astype(jnp.bfloat16)
    keys = keys.reshape(batch, row_count, head_cols)
    values = values.reshape(batch, row_count, head_cols)
    query_length = lengths[0, :, 0]
    key_length = lengths[0, :, 1]
    split_queries = queries.reshape(batch, row_count, local_heads, DH)
    key_piece = lax.all_gather(keys, "seq", axis=1, tiled=True)
    value_piece = lax.all_gather(values, "seq", axis=1, tiled=True)
    key_count = key_piece.shape[1]
    scores = (
        jnp.einsum(
            "bqhd,bkhd->bqhk",
            split_queries,
            key_piece.reshape(batch, key_count, local_heads, DH),
            preferred_element_type=jnp.float32,
        )
        * 0.25
    )
    visible = jnp.arange(key_count)[None, :] < key_length[:, None]
    mask = visible[:, None, None, :]
    scores = jnp.where(mask, scores, -1e30)
    largest = jnp.max(scores, axis=-1)
    exponent = jnp.where(mask, jnp.exp(scores - largest[..., None]), 0.0)
    totals = jnp.sum(exponent, axis=-1)
    weighted = jnp.einsum(
        "bqhk,bkhd->bqhd",
        exponent.astype(jnp.bfloat16),
        value_piece.reshape(batch, key_count, local_heads, DH),
        preferred_element_type=jnp.float32,
    )
    context = weighted / totals[..., None]
    positions = lax.axis_index("seq") * row_count + jnp.arange(row_count)
    live_rows = positions[None, :] < query_length[:, None]
    context = jnp.where(live_rows[:, :, None, None], context, 0.0)
    context = context.astype(jnp.bfloat16).reshape(batch * row_count, head_cols)
    partial_value = jnp.dot(context, w_out[0], preferred_element_type=jnp.float32)
    branch = lax.psum_scatter(
        partial_value.astype(jnp.bfloat16), "mp", scatter_dimension=1, tiled=True
    ).astype(jnp.float32)
    branch = branch.reshape(batch, row_count, branch.shape[1])
    return (own_part.astype(jnp.float32) + branch).astype(jnp.bfloat16)[None]


HEAD, SIDE, INNER, ENC = 0, 1, 2, 3
BLOCK = 4


def in_vmem(array):
    return pltpu.with_memory_space_constraint(array, pltpu.VMEM)


def in_hbm(array):
    return pltpu.with_memory_space_constraint(array, pltpu.HBM)


def split_kernel(table, hidden, memory, own, away, sems):
    inner = table[INNER]

    def copied(array):
        copies = [
            pltpu.make_async_copy(array.at[0, inner], own, sems.at[0]),
            pltpu.make_async_copy(array.at[0, 1 - inner], away, sems.at[1]),
        ]
        for copy in copies:
            copy.start()
        for copy in copies:
            copy.wait()

    if memory is None:
        copied(hidden)
    else:
        pl.when(table[ENC] == 1)(lambda: copied(hidden))
        pl.when(table[ENC] == 0)(lambda: copied(memory))


def split(table, hidden, memory=None):
    arrays = [hidden] if memory is None else [hidden, memory]

    def kernel(table, hidden, *rest):
        split_kernel(table, hidden, *([None] if memory is None else []), *rest)

    return pl.pallas_call(
        kernel,
        out_shape=[jax.ShapeDtypeStruct(hidden.shape[2:], jnp.bfloat16)] * 2,
        in_specs=[pl.BlockSpec(memory_space=pltpu.SMEM), pl.BlockSpec(memory_space=pltpu.HBM)]
        + [pl.BlockSpec(memory_space=pl.ANY)] * (len(arrays) - 1),
        out_specs=[IN_VMEM] * 2,
        scratch_shapes=[pltpu.SemaphoreType.DMA((2,))],
        compiler_params=pltpu.CompilerParams(vmem_limit_bytes=4 * MIB),
        cost_estimate=SMALL,
    )(table, in_hbm(hidden), *arrays[1:])


def mark(array):
    def kernel(array, out):
        out[...] = jnp.zeros(out.shape, out.dtype)

    return pl.pallas_call(
        kernel,
        out_shape=jax.ShapeDtypeStruct((8, LANES), jnp.float32),
        in_specs=[pl.BlockSpec(memory_space=pl.ANY)],
        out_specs=IN_VMEM,
        compiler_params=pltpu.CompilerParams(vmem_limit_bytes=MIB),
        cost_estimate=pl.CostEstimate(flops=0, bytes_accessed=8 * MIB, transcendentals=0),
    )(array)


def times_gain(values, gains, side, into):
    half = values.shape[1]
    wide = values.astype(jnp.float32)
    into[...] = (wide * gains[:, pl.ds(pl.multiple_of(side * half, half), half)]).astype(jnp.bfloat16)
    return jnp.sum(wide * wide, axis=-1, keepdims=True)


def row_factor(total, features):
    return lax.rsqrt(total / features + 1e-06)


def fetch_kernel(count, *refs):
    sources, targets, sems = refs[:count], refs[count:-1], refs[-1]
    copies = [
        pltpu.make_async_copy(source.at[0], target, sems.at[n])
        for n, (source, target) in enumerate(zip(sources, targets))
    ]
    for copy in copies:
        copy.start()
    for copy in copies:
        copy.wait()


def fetch(weights):
    return pl.pallas_call(
        functools.partial(fetch_kernel, len(weights)),
        out_shape=[pltpu.VMEM(weight.shape[1:], jnp.bfloat16) for weight in weights],
        in_specs=[pl.BlockSpec(memory_space=pltpu.HBM)] * len(weights),
        out_specs=[IN_VMEM] * len(weights),
        scratch_shapes=[pltpu.SemaphoreType.DMA((len(weights),))],
        compiler_params=pltpu.CompilerParams(vmem_limit_bytes=2 * MIB),
        cost_estimate=SMALL,
    )(*[in_hbm(weight) for weight in weights])


def project_kernel(count, queried, table, *refs):
    size = 4 if queried else 2
    (gain, last_gain), weights, rest = refs[size : size + 2], refs[size + 2 : size + 5], refs[size + 5 :]
    outs, (xk, xq, fk, fq) = rest[:count], rest[-4:]
    side = table[SIDE]
    rows, half = refs[0].shape
    width = weights[0].shape[1] // count

    def fill(own, other, gains, x, f):
        total = times_gain(own, gains, side, x.at[0]) + times_gain(other, gains, 1 - side, x.at[1])
        f[...] = jnp.broadcast_to(row_factor(total, 2 * half), (rows, LANES))

    if queried:
        qo, qn, ko, kn = refs[:4]
        fill(qo[...], qn[...], gain, xq, fq)

        @pl.when(table[ENC] == 1)
        def _():
            xk[...] = xq[...]
            fk[...] = fq[...]

    else:
        ko, kn = refs[:2]

        @pl.when(table[ENC] == 1)
        def _():
            fill(ko[...], kn[...], gain, xk, fk)

    @pl.when(table[ENC] == 0)
    def _():
        fill(ko[...], kn[...], last_gain, xk, fk)

    def part(s):
        return pl.ds(pl.multiple_of(s * half, half), half)

    for n in range(3 if queried else 2):
        x, f = (xq, fq) if n == 2 else (xk, fk)
        scale = f[:, :1] * SCALE if n == 2 else f[:, :1]
        for turn in range(count - 1, -1, -1):
            columns = pl.ds(pl.multiple_of((table[HEAD] ^ turn) * width, width), width)
            total = jnp.dot(x[0], weights[n][part(side), columns], preferred_element_type=jnp.float32)
            total += jnp.dot(x[1], weights[n][part(1 - side), columns], preferred_element_type=jnp.float32)
            outs[turn][:, n * width : (n + 1) * width] = (total * scale).astype(jnp.bfloat16)


def project(table, arrays, gains, weights, count):
    rows, half = arrays[0].shape
    columns = weights[0].shape[1]
    queried = len(arrays) == 4
    width = (3 if queried else 2) * columns // count
    first = 1 + len(arrays) + 2
    products = pl.pallas_call(
        functools.partial(project_kernel, count, queried),
        out_shape=[jax.ShapeDtypeStruct((rows, width), jnp.bfloat16)] * count
        + [pltpu.VMEM(weight.shape, jnp.bfloat16) for weight in weights],
        grid_spec=pltpu.PrefetchScalarGridSpec(
            num_scalar_prefetch=1,
            grid=(1,),
            in_specs=[IN_VMEM] * (len(arrays) + 2 + len(weights)),
            out_specs=[IN_VMEM] * (count + len(weights)),
            scratch_shapes=[pltpu.VMEM((2, rows, half), jnp.bfloat16)] * 2
            + [pltpu.VMEM((rows, LANES), jnp.float32)] * 2,
        ),
        input_output_aliases={first + n: count + n for n in range(len(weights))},
        compiler_params=pltpu.CompilerParams(vmem_limit_bytes=8 * MIB),
        cost_estimate=SMALL,
    )(table, *arrays, *gains, *[in_vmem(weight) for weight in weights])
    return products[:count], products[count:]


def attend_kernel(chosen, tile, blocks, table, lengths, *refs):
    arrays, outs, (qs, ks, vs, contexts) = refs[:blocks], refs[blocks:-4], refs[-4:]
    rows, width = outs[0].shape
    pairs = width // LANES
    query_length = lengths[2 * table[INNER]]
    key_length = lengths[2 * table[INNER] + 1]
    lane = lax.broadcasted_iota(jnp.int32, (rows, LANES), 1)
    row = lax.broadcasted_iota(jnp.int32, (rows, LANES), 0)
    low = lane < DH
    zero = jnp.zeros((rows, LANES), jnp.bfloat16)
    one = jnp.ones((rows, LANES), jnp.bfloat16)
    unit = jnp.where(lane == 0, one, zero)

    def lanes(block):
        return slice(block * LANES, (block + 1) * LANES)

    for j in range(blocks):
        here = pl.ds(j * rows, rows)
        hides = jnp.logical_and(lane == 0, row + table[BLOCK + j] >= key_length)
        bias = jnp.where(hides, -1e30, 0.0).astype(jnp.bfloat16)
        for pair in range(pairs):
            key = arrays[j][:, lanes(pair)]
            value = arrays[j][:, lanes(pairs + pair)]
            ks[pair, 0, here, :LANES] = jnp.where(low, key, zero)
            ks[pair, 1, here, :LANES] = jnp.where(low, zero, key)
            ks[pair, 0, here, LANES:] = bias
            ks[pair, 1, here, LANES:] = bias
            vs[pair, 0, here, :] = jnp.where(low, value, one)
            vs[pair, 1, here, :] = jnp.where(low, one, value)
    for i, j in enumerate(chosen):
        here = pl.ds(i * rows, rows)
        for pair in range(pairs):
            qs[pair, here, :LANES] = arrays[j][:, lanes(2 * pairs + pair)]
            qs[pair, here, LANES:] = unit

    low = lax.broadcasted_iota(jnp.int32, (tile, LANES), 1) < DH
    for pair in range(pairs):
        for t in range(len(chosen) * rows // tile):
            here = pl.ds(t * tile, tile)
            sums = []
            for head in range(2):
                scores = lax.dot_general(
                    qs[pair, here, :], ks[pair, head], (((1,), (1,)), ((), ())), preferred_element_type=jnp.float32
                )
                largest = jnp.max(scores, axis=-1, keepdims=True)
                weights = jnp.exp2(scores - largest).astype(jnp.bfloat16)
                sums.append(jnp.dot(weights, vs[pair, head], preferred_element_type=jnp.float32))
            weighted = jnp.where(low, sums[0], sums[1])
            totals = jnp.where(low, pltpu.roll(sums[0], DH, 1), pltpu.roll(sums[1], DH, 1))
            contexts[here, lanes(pair)] = (weighted / totals).astype(jnp.bfloat16)

    for i, j in enumerate(chosen):
        live = row + table[BLOCK + j] < query_length
        for pair in range(pairs):
            outs[i][:, lanes(pair)] = jnp.where(live, contexts[pl.ds(i * rows, rows), lanes(pair)], zero)


def attend(table, lengths, arrays, chosen, width):
    rows = arrays[0].shape[0]
    total = len(arrays) * rows
    size = len(chosen) * rows
    pairs = width // LANES
    return pl.pallas_call(
        functools.partial(attend_kernel, chosen, size, len(arrays)),
        out_shape=[jax.ShapeDtypeStruct((rows, width), jnp.bfloat16)] * len(chosen),
        grid_spec=pltpu.PrefetchScalarGridSpec(
            num_scalar_prefetch=2,
            grid=(1,),
            in_specs=[IN_VMEM] * len(arrays),
            out_specs=[IN_VMEM] * len(chosen),
            scratch_shapes=[
                pltpu.VMEM((pairs, size, 2 * LANES), jnp.bfloat16),
                pltpu.VMEM((pairs, 2, total, 2 * LANES), jnp.bfloat16),
                pltpu.VMEM((pairs, 2, total, LANES), jnp.bfloat16),
                pltpu.VMEM((size, width), jnp.bfloat16),
            ],
        ),
        compiler_params=pltpu.CompilerParams(vmem_limit_bytes=32 * MIB),
        cost_estimate=SMALL,
    )(table, lengths, *arrays)


def output_kernel(count, table, w, *refs):
    pieces, outs, x = refs[:count], refs[count : count + 2], refs[-1]
    width = pieces[0].shape[1]
    half = outs[0].shape[1]
    for turn in range(count):
        place = pl.multiple_of((table[HEAD] ^ turn) * width, width)
        x[:, pl.ds(place, width)] = pieces[turn][...]
    for i in range(2):
        columns = pl.ds(pl.multiple_of((1 - (table[SIDE] ^ i)) * half, half), half)
        outs[i][...] = jnp.dot(x[...], w[:, columns], preferred_element_type=jnp.float32).astype(jnp.bfloat16)


def output_parts(table, pieces, w_out):
    rows, width = pieces[0].shape
    depth, half = w_out.shape[0], w_out.shape[1] // 2
    return pl.pallas_call(
        functools.partial(output_kernel, len(pieces)),
        out_shape=[jax.ShapeDtypeStruct((rows, half), jnp.bfloat16)] * 2,
        grid_spec=pltpu.PrefetchScalarGridSpec(
            num_scalar_prefetch=1,
            grid=(1,),
            in_specs=[IN_VMEM] * (1 + len(pieces)),
            out_specs=[IN_VMEM] * 2,
            scratch_shapes=[pltpu.VMEM((rows, depth), jnp.bfloat16)],
        ),
        compiler_params=pltpu.CompilerParams(vmem_limit_bytes=16 * MIB),
        cost_estimate=SMALL,
    )(table, w_out, *pieces)


def add_kernel(table, hidden, own, beside, across, corner, out):
    def total(a, b):
        out[0, 0] = (
            hidden[0, 0].astype(jnp.float32) + (a[...].astype(jnp.float32) + b[...].astype(jnp.float32))
        ).astype(jnp.bfloat16)

    @pl.when(pl.program_id(0) == 0)
    def _():
        total(own, beside)

    @pl.when(pl.program_id(0) == 1)
    def _():
        total(across, corner)


def add_all(table, hidden, own, beside, across, corner):
    rows, half = own.shape
    block = pl.BlockSpec((1, 1, rows, half), lambda i, table: (0, table[INNER] ^ i, 0, 0))
    part = pl.BlockSpec((rows, half), lambda i, table: (0, 0))
    return pl.pallas_call(
        add_kernel,
        out_shape=jax.ShapeDtypeStruct(hidden.shape, jnp.bfloat16),
        grid_spec=pltpu.PrefetchScalarGridSpec(
            num_scalar_prefetch=1,
            grid=(2,),
            in_specs=[block, part, part, part, part],
            out_specs=block,
        ),
        compiler_params=pltpu.CompilerParams(vmem_limit_bytes=16 * MIB),
    )(table, hidden, own, beside, across, corner)


def body(hidden, memory, w_query, w_key, w_value, w_out, norm_gain, final_gain, lengths):
    seq, mp = lax.axis_size("seq"), lax.axis_size("mp")
    width = w_query.shape[2] // 2
    rows = hidden.shape[2]

    place, side = lax.axis_index("seq"), lax.axis_index("mp")
    encoder = (lax.axis_index("segment") == 0).astype(jnp.int32)
    chunks = range(0, seq, 2)
    starts = [(place ^ (chunk + turn)) * rows for chunk in chunks for turn in range(2)]
    table = jnp.stack([place % 2, side, place // 2 % 2, encoder] + starts).astype(jnp.int32)

    def moved(value, swap_seq, swap_mp, segments=(0, 1)):
        pairs = [
            ((g * seq + s) * mp + m, (g * seq + (s ^ swap_seq)) * mp + (m ^ swap_mp))
            for g in segments
            for s in range(seq)
            for m in range(mp)
        ]
        return lax.ppermute(value, ("segment", "seq", "mp"), pairs)

    def after(value, *others):
        return lax.optimization_barrier((value, *others))[0]

    gains = (in_hbm(norm_gain), in_hbm(final_gain.reshape(1, -1)))
    weights = (w_key, w_value, w_query)

    arrived = passed_along(memory[0], "segment", 1)
    hidden_own, hidden_away = split(table, hidden)
    query = {0: hidden_own}
    query_other = {0: moved(hidden_own, 0, 1)}
    query[2] = moved(hidden_away, 2, 0)
    source_own, source_away = split(table, hidden, after(arrived, hidden_own)[None])
    source = {0: source_own}
    source_other = {0: moved(source_own, 0, 1, (1,))}
    source[2] = moved(source_away, 2, 0, (1,))
    if seq > 4:
        source[4] = moved(source_own, 4, 0)
    held = [fetch([after(weight, query_other[0]) for weight in weights])]
    query_other[2] = moved(after(query[2], held[0]), 0, 1)
    source_other[2] = moved(after(source[2], held[0]), 0, 1, (1,))

    def projected(chunk, *others):
        parts = [source[chunk], source_other[chunk]]
        if chunk < 4:
            parts = [query[chunk], query_other[chunk]] + parts
        parts[0] = after(parts[0], *others)
        (kept, sent), held[0] = project(table, parts, gains, held[0], 2)
        return kept, moved(sent, 1, 0)

    done = {0: projected(0, query[2], source[2])}
    before = done[0][0]
    if seq > 4:
        source[4] = after(source[4], before)
        source_other[4] = moved(source[4], 0, 1)
        before = [before, mark(source[4])]
    last = before
    for chunk in chunks[3:]:
        source[chunk] = moved(after(source_away if chunk & 2 else source_own, last), chunk, 0)
        last = source[chunk]
    done[2] = projected(2, before)
    before = done[2][0]
    for chunk in chunks[2:]:
        if chunk > 4:
            source_other[chunk] = moved(after(source[chunk], done[2][0]), 0, 1)
        done[chunk] = projected(chunk, before, done[chunk - 4][1])
        before = done[chunk][0]
    arrays = [array for chunk in chunks for array in done[chunk]]

    lengths = lengths.reshape(-1)
    context = attend(table, lengths, arrays, (0, 1), width)
    first_context = [context[0], moved(context[1], 1, 0)]
    context = attend(table, lengths, after(arrays, context), (2, 3), width)
    second_context = [moved(after(context[turn], first_context[1]), 2 + turn, 0) for turn in range(2)]
    away, own = output_parts(table, first_context, w_out[0])
    first_beside = moved(away, 0, 1)
    away, second_own = output_parts(table, second_context, w_out[0])
    second_beside = moved(away, 0, 1)
    return add_all(table, hidden, own, first_beside, second_own, second_beside)


def solution(mesh):
    seq, mp = mesh.shape["seq"], mesh.shape["mp"]

    def chosen(*arrays):
        batch, columns = arrays[0].shape[1], arrays[2].shape[2]
        fits = (
            batch == 2
            and mp == 2
            and seq >= 4
            and seq & (seq - 1) == 0
            and (columns // mp) % (2 * LANES) == 0
            and (arrays[0].shape[2] // seq) % 16 == 0
        )
        return jax.shard_map(
            body if fits else gathered_body,
            mesh=mesh,
            in_specs=(
                P("segment", None, "seq", "mp"),
                P("segment", None, "seq", "mp"),
                P("segment", None, "mp"),
                P("segment", None, "mp"),
                P("segment", None, "mp"),
                P("segment", "mp", None),
                P("segment", None),
                P(),
                P("segment", None, None),
            ),
            out_specs=P("segment", None, "seq", "mp"),
            check_vma=False,
        )(*arrays)

    return chosen
```

```python
import functools

import jax
import jax.numpy as jnp
from jax import lax
from jax.experimental import pallas as pl
from jax.experimental.pallas import tpu as pltpu
from jax.sharding import PartitionSpec as P

DH = 64
LANES = 128
SCALE = 0.25 * 1.4426950408889634
MIB = 1024 * 1024
SMALL = pl.CostEstimate(flops=1, bytes_accessed=1, transcendentals=0)
IN_VMEM = pl.BlockSpec(memory_space=pltpu.VMEM)


def passed_along(value, axis, steps):
    count = lax.axis_size(axis)
    leading, last = (max(0, -steps), min(count, count - steps))
    return lax.ppermute(value, axis, [(source, source + steps) for source in range(leading, last)])


def normalize(values, gain_row):
    widened = values.astype(jnp.float32)
    square = jnp.mean(widened * widened, axis=-1, keepdims=True)
    return (widened * lax.rsqrt(square + 1e-06) * gain_row).astype(jnp.bfloat16)


def gathered_body(hidden, memory, w_query, w_key, w_value, w_out, norm_gain, final_gain, lengths):
    encoder_side = lax.axis_index("segment") == 0
    own_part = hidden[0]
    arrived = passed_along(memory[0], "segment", 1)
    source_part = jnp.where(encoder_side, own_part, arrived)
    query_rows, source_rows = (
        lax.all_gather(own_part, "mp", axis=2, tiled=True),
        lax.all_gather(source_part, "mp", axis=2, tiled=True),
    )
    batch = own_part.shape[0]
    row_count = own_part.shape[1]
    width = query_rows.shape[2]
    key_gain = jnp.where(encoder_side, norm_gain[0], final_gain)
    query_in = normalize(query_rows.reshape(batch * row_count, width), norm_gain[0])
    key_in = normalize(source_rows.reshape(batch * row_count, width), key_gain)
    head_cols = w_query.shape[2]
    local_heads = head_cols // DH
    queries = jnp.dot(query_in, w_query[0], preferred_element_type=jnp.float32).astype(jnp.bfloat16)
    keys = jnp.dot(key_in, w_key[0], preferred_element_type=jnp.float32).astype(jnp.bfloat16)
    values = jnp.dot(key_in, w_value[0], preferred_element_type=jnp.float32).astype(jnp.bfloat16)
    keys = keys.reshape(batch, row_count, head_cols)
    values = values.reshape(batch, row_count, head_cols)
    query_length = lengths[0, :, 0]
    key_length = lengths[0, :, 1]
    split_queries = queries.reshape(batch, row_count, local_heads, DH)
    key_piece = lax.all_gather(keys, "seq", axis=1, tiled=True)
    value_piece = lax.all_gather(values, "seq", axis=1, tiled=True)
    key_count = key_piece.shape[1]
    scores = (
        jnp.einsum(
            "bqhd,bkhd->bqhk",
            split_queries,
            key_piece.reshape(batch, key_count, local_heads, DH),
            preferred_element_type=jnp.float32,
        )
        * 0.25
    )
    visible = jnp.arange(key_count)[None, :] < key_length[:, None]
    mask = visible[:, None, None, :]
    scores = jnp.where(mask, scores, -1e30)
    largest = jnp.max(scores, axis=-1)
    exponent = jnp.where(mask, jnp.exp(scores - largest[..., None]), 0.0)
    totals = jnp.sum(exponent, axis=-1)
    weighted = jnp.einsum(
        "bqhk,bkhd->bqhd",
        exponent.astype(jnp.bfloat16),
        value_piece.reshape(batch, key_count, local_heads, DH),
        preferred_element_type=jnp.float32,
    )
    context = weighted / totals[..., None]
    positions = lax.axis_index("seq") * row_count + jnp.arange(row_count)
    live_rows = positions[None, :] < query_length[:, None]
    context = jnp.where(live_rows[:, :, None, None], context, 0.0)
    context = context.astype(jnp.bfloat16).reshape(batch * row_count, head_cols)
    partial_value = jnp.dot(context, w_out[0], preferred_element_type=jnp.float32)
    branch = lax.psum_scatter(
        partial_value.astype(jnp.bfloat16), "mp", scatter_dimension=1, tiled=True
    ).astype(jnp.float32)
    branch = branch.reshape(batch, row_count, branch.shape[1])
    return (own_part.astype(jnp.float32) + branch).astype(jnp.bfloat16)[None]


HEAD, SIDE, INNER, ENC = 0, 1, 2, 3
BLOCK = 4


def in_vmem(array):
    return pltpu.with_memory_space_constraint(array, pltpu.VMEM)


def in_hbm(array):
    return pltpu.with_memory_space_constraint(array, pltpu.HBM)


def split_kernel(table, hidden, memory, own, away, sems):
    inner = table[INNER]

    def copied(array):
        copies = [
            pltpu.make_async_copy(array.at[0, inner], own, sems.at[0]),
            pltpu.make_async_copy(array.at[0, 1 - inner], away, sems.at[1]),
        ]
        for copy in copies:
            copy.start()
        for copy in copies:
            copy.wait()

    if memory is None:
        copied(hidden)
    else:
        pl.when(table[ENC] == 1)(lambda: copied(hidden))
        pl.when(table[ENC] == 0)(lambda: copied(memory))


def split(table, hidden, memory=None):
    arrays = [hidden] if memory is None else [hidden, memory]

    def kernel(table, hidden, *rest):
        split_kernel(table, hidden, *([None] if memory is None else []), *rest)

    return pl.pallas_call(
        kernel,
        out_shape=[jax.ShapeDtypeStruct(hidden.shape[2:], jnp.bfloat16)] * 2,
        in_specs=[pl.BlockSpec(memory_space=pltpu.SMEM), pl.BlockSpec(memory_space=pltpu.HBM)]
        + [pl.BlockSpec(memory_space=pl.ANY)] * (len(arrays) - 1),
        out_specs=[IN_VMEM] * 2,
        scratch_shapes=[pltpu.SemaphoreType.DMA((2,))],
        compiler_params=pltpu.CompilerParams(vmem_limit_bytes=4 * MIB),
        cost_estimate=SMALL,
    )(table, in_hbm(hidden), *arrays[1:])


def times_gain(values, gains, side, into):
    half = values.shape[1]
    wide = values.astype(jnp.float32)
    into[...] = (wide * gains[:, pl.ds(pl.multiple_of(side * half, half), half)]).astype(jnp.bfloat16)
    return jnp.sum(wide * wide, axis=-1, keepdims=True)


def row_factor(total, features):
    return lax.rsqrt(total / features + 1e-06)


def fetch_kernel(count, *refs):
    sources, targets, sems = refs[:count], refs[count:-1], refs[-1]
    copies = [
        pltpu.make_async_copy(source.at[0], target, sems.at[n])
        for n, (source, target) in enumerate(zip(sources, targets))
    ]
    for copy in copies:
        copy.start()
    for copy in copies:
        copy.wait()


def fetch(weights):
    return pl.pallas_call(
        functools.partial(fetch_kernel, len(weights)),
        out_shape=[pltpu.VMEM(weight.shape[1:], jnp.bfloat16) for weight in weights],
        in_specs=[pl.BlockSpec(memory_space=pltpu.HBM)] * len(weights),
        out_specs=[IN_VMEM] * len(weights),
        scratch_shapes=[pltpu.SemaphoreType.DMA((len(weights),))],
        compiler_params=pltpu.CompilerParams(vmem_limit_bytes=2 * MIB),
        cost_estimate=SMALL,
    )(*[in_hbm(weight) for weight in weights])


def project_kernel(count, queried, table, *refs):
    size = 4 if queried else 2
    (gain, last_gain), weights, rest = refs[size : size + 2], refs[size + 2 : size + 5], refs[size + 5 :]
    outs, (xk, xq, fk, fq) = rest[:count], rest[-4:]
    side = table[SIDE]
    rows, half = refs[0].shape
    width = weights[0].shape[1] // count

    def fill(own, other, gains, x, f):
        total = times_gain(own, gains, side, x.at[0]) + times_gain(other, gains, 1 - side, x.at[1])
        f[...] = jnp.broadcast_to(row_factor(total, 2 * half), (rows, LANES))

    if queried:
        qo, qn, ko, kn = refs[:4]
        fill(qo[...], qn[...], gain, xq, fq)

        @pl.when(table[ENC] == 1)
        def _():
            xk[...] = xq[...]
            fk[...] = fq[...]

    else:
        ko, kn = refs[:2]

        @pl.when(table[ENC] == 1)
        def _():
            fill(ko[...], kn[...], gain, xk, fk)

    @pl.when(table[ENC] == 0)
    def _():
        fill(ko[...], kn[...], last_gain, xk, fk)

    def part(s):
        return pl.ds(pl.multiple_of(s * half, half), half)

    for n in range(3 if queried else 2):
        x, f = (xq, fq) if n == 2 else (xk, fk)
        scale = f[:, :1] * SCALE if n == 2 else f[:, :1]
        for turn in range(count - 1, -1, -1):
            columns = pl.ds(pl.multiple_of((table[HEAD] ^ turn) * width, width), width)
            total = jnp.dot(x[0], weights[n][part(side), columns], preferred_element_type=jnp.float32)
            total += jnp.dot(x[1], weights[n][part(1 - side), columns], preferred_element_type=jnp.float32)
            outs[turn][:, n * width : (n + 1) * width] = (total * scale).astype(jnp.bfloat16)


def project(table, arrays, gains, weights, count):
    rows, half = arrays[0].shape
    columns = weights[0].shape[1]
    queried = len(arrays) == 4
    width = (3 if queried else 2) * columns // count
    first = 1 + len(arrays) + 2
    products = pl.pallas_call(
        functools.partial(project_kernel, count, queried),
        out_shape=[jax.ShapeDtypeStruct((rows, width), jnp.bfloat16)] * count
        + [pltpu.VMEM(weight.shape, jnp.bfloat16) for weight in weights],
        grid_spec=pltpu.PrefetchScalarGridSpec(
            num_scalar_prefetch=1,
            grid=(1,),
            in_specs=[IN_VMEM] * (len(arrays) + 2 + len(weights)),
            out_specs=[IN_VMEM] * (count + len(weights)),
            scratch_shapes=[pltpu.VMEM((2, rows, half), jnp.bfloat16)] * 2
            + [pltpu.VMEM((rows, LANES), jnp.float32)] * 2,
        ),
        input_output_aliases={first + n: count + n for n in range(len(weights))},
        compiler_params=pltpu.CompilerParams(vmem_limit_bytes=8 * MIB),
        cost_estimate=SMALL,
    )(table, *arrays, *gains, *[in_vmem(weight) for weight in weights])
    return products[:count], products[count:]


def attend_kernel(chosen, tile, blocks, table, lengths, *refs):
    arrays, outs, (qs, ks, vs, contexts) = refs[:blocks], refs[blocks:-4], refs[-4:]
    rows, width = outs[0].shape
    pairs = width // LANES
    query_length = lengths[2 * table[INNER]]
    key_length = lengths[2 * table[INNER] + 1]
    lane = lax.broadcasted_iota(jnp.int32, (rows, LANES), 1)
    row = lax.broadcasted_iota(jnp.int32, (rows, LANES), 0)
    low = lane < DH
    zero = jnp.zeros((rows, LANES), jnp.bfloat16)
    one = jnp.ones((rows, LANES), jnp.bfloat16)
    unit = jnp.where(lane == 0, one, zero)

    def lanes(block):
        return slice(block * LANES, (block + 1) * LANES)

    for j in range(blocks):
        here = pl.ds(j * rows, rows)
        hides = jnp.logical_and(lane == 0, row + table[BLOCK + j] >= key_length)
        bias = jnp.where(hides, -1e30, 0.0).astype(jnp.bfloat16)
        for pair in range(pairs):
            key = arrays[j][:, lanes(pair)]
            value = arrays[j][:, lanes(pairs + pair)]
            ks[pair, 0, here, :LANES] = jnp.where(low, key, zero)
            ks[pair, 1, here, :LANES] = jnp.where(low, zero, key)
            ks[pair, 0, here, LANES:] = bias
            ks[pair, 1, here, LANES:] = bias
            vs[pair, 0, here, :] = jnp.where(low, value, one)
            vs[pair, 1, here, :] = jnp.where(low, one, value)
    for i, j in enumerate(chosen):
        here = pl.ds(i * rows, rows)
        for pair in range(pairs):
            qs[pair, here, :LANES] = arrays[j][:, lanes(2 * pairs + pair)]
            qs[pair, here, LANES:] = unit

    low = lax.broadcasted_iota(jnp.int32, (tile, LANES), 1) < DH
    for pair in range(pairs):
        for t in range(len(chosen) * rows // tile):
            here = pl.ds(t * tile, tile)
            sums = []
            for head in range(2):
                scores = lax.dot_general(
                    qs[pair, here, :], ks[pair, head], (((1,), (1,)), ((), ())), preferred_element_type=jnp.float32
                )
                largest = jnp.max(scores, axis=-1, keepdims=True)
                weights = jnp.exp2(scores - largest).astype(jnp.bfloat16)
                sums.append(jnp.dot(weights, vs[pair, head], preferred_element_type=jnp.float32))
            weighted = jnp.where(low, sums[0], sums[1])
            totals = jnp.where(low, pltpu.roll(sums[0], DH, 1), pltpu.roll(sums[1], DH, 1))
            contexts[here, lanes(pair)] = (weighted / totals).astype(jnp.bfloat16)

    for i, j in enumerate(chosen):
        live = row + table[BLOCK + j] < query_length
        for pair in range(pairs):
            outs[i][:, lanes(pair)] = jnp.where(live, contexts[pl.ds(i * rows, rows), lanes(pair)], zero)


def attend(table, lengths, arrays, chosen, width):
    rows = arrays[0].shape[0]
    total = len(arrays) * rows
    size = len(chosen) * rows
    pairs = width // LANES
    return pl.pallas_call(
        functools.partial(attend_kernel, chosen, size, len(arrays)),
        out_shape=[jax.ShapeDtypeStruct((rows, width), jnp.bfloat16)] * len(chosen),
        grid_spec=pltpu.PrefetchScalarGridSpec(
            num_scalar_prefetch=2,
            grid=(1,),
            in_specs=[IN_VMEM] * len(arrays),
            out_specs=[IN_VMEM] * len(chosen),
            scratch_shapes=[
                pltpu.VMEM((pairs, size, 2 * LANES), jnp.bfloat16),
                pltpu.VMEM((pairs, 2, total, 2 * LANES), jnp.bfloat16),
                pltpu.VMEM((pairs, 2, total, LANES), jnp.bfloat16),
                pltpu.VMEM((size, width), jnp.bfloat16),
            ],
        ),
        compiler_params=pltpu.CompilerParams(vmem_limit_bytes=32 * MIB),
        cost_estimate=SMALL,
    )(table, lengths, *arrays)


def output_kernel(count, table, w, *refs):
    pieces, outs, x = refs[:count], refs[count : count + 2], refs[-1]
    width = pieces[0].shape[1]
    half = outs[0].shape[1]
    for turn in range(count):
        place = pl.multiple_of((table[HEAD] ^ turn) * width, width)
        x[:, pl.ds(place, width)] = pieces[turn][...]
    for i in range(2):
        columns = pl.ds(pl.multiple_of((1 - (table[SIDE] ^ i)) * half, half), half)
        outs[i][...] = jnp.dot(x[...], w[:, columns], preferred_element_type=jnp.float32).astype(jnp.bfloat16)


def output_parts(table, pieces, w_out):
    rows, width = pieces[0].shape
    depth, half = w_out.shape[0], w_out.shape[1] // 2
    return pl.pallas_call(
        functools.partial(output_kernel, len(pieces)),
        out_shape=[jax.ShapeDtypeStruct((rows, half), jnp.bfloat16)] * 2,
        grid_spec=pltpu.PrefetchScalarGridSpec(
            num_scalar_prefetch=1,
            grid=(1,),
            in_specs=[IN_VMEM] * (1 + len(pieces)),
            out_specs=[IN_VMEM] * 2,
            scratch_shapes=[pltpu.VMEM((rows, depth), jnp.bfloat16)],
        ),
        compiler_params=pltpu.CompilerParams(vmem_limit_bytes=16 * MIB),
        cost_estimate=SMALL,
    )(table, w_out, *pieces)


def add_kernel(table, hidden, own, beside, across, corner, out):
    def total(a, b):
        out[0, 0] = (
            hidden[0, 0].astype(jnp.float32) + (a[...].astype(jnp.float32) + b[...].astype(jnp.float32))
        ).astype(jnp.bfloat16)

    @pl.when(pl.program_id(0) == 0)
    def _():
        total(own, beside)

    @pl.when(pl.program_id(0) == 1)
    def _():
        total(across, corner)


def add_all(table, hidden, own, beside, across, corner):
    rows, half = own.shape
    block = pl.BlockSpec((1, 1, rows, half), lambda i, table: (0, table[INNER] ^ i, 0, 0))
    part = pl.BlockSpec((rows, half), lambda i, table: (0, 0))
    return pl.pallas_call(
        add_kernel,
        out_shape=jax.ShapeDtypeStruct(hidden.shape, jnp.bfloat16),
        grid_spec=pltpu.PrefetchScalarGridSpec(
            num_scalar_prefetch=1,
            grid=(2,),
            in_specs=[block, part, part, part, part],
            out_specs=block,
        ),
        compiler_params=pltpu.CompilerParams(vmem_limit_bytes=16 * MIB),
    )(table, hidden, own, beside, across, corner)


def body(hidden, memory, w_query, w_key, w_value, w_out, norm_gain, final_gain, lengths):
    seq, mp = lax.axis_size("seq"), lax.axis_size("mp")
    width = w_query.shape[2] // 2
    rows = hidden.shape[2]

    place, side = lax.axis_index("seq"), lax.axis_index("mp")
    encoder = (lax.axis_index("segment") == 0).astype(jnp.int32)
    chunks = range(0, seq, 2)
    starts = [(place ^ (chunk + turn)) * rows for chunk in chunks for turn in range(2)]
    table = jnp.stack([place % 2, side, place // 2 % 2, encoder] + starts).astype(jnp.int32)

    def moved(value, swap_seq, swap_mp, segments=(0, 1)):
        pairs = [
            ((g * seq + s) * mp + m, (g * seq + (s ^ swap_seq)) * mp + (m ^ swap_mp))
            for g in segments
            for s in range(seq)
            for m in range(mp)
        ]
        return lax.ppermute(value, ("segment", "seq", "mp"), pairs)

    def after(value, *others):
        return lax.optimization_barrier((value, *others))[0]

    gains = (in_hbm(norm_gain), in_hbm(final_gain.reshape(1, -1)))
    weights = (w_key, w_value, w_query)

    arrived = passed_along(memory[0], "segment", 1)
    hidden_own, hidden_away = split(table, hidden)
    query = {0: hidden_own}
    query_other = {0: moved(hidden_own, 0, 1)}
    query[2] = moved(hidden_away, 2, 0)
    source_own, source_away = split(table, hidden, after(arrived, hidden_own)[None])
    source = {0: source_own}
    source_other = {0: moved(source_own, 0, 1, (1,))}
    source[2] = moved(source_away, 2, 0, (1,))
    if seq > 4:
        source[4] = moved(after(source_own, query_other[0]), 4, 0)
    held = [fetch([after(weight, query_other[0]) for weight in weights])]
    query_other[2] = moved(after(query[2], held[0]), 0, 1)
    source_other[2] = moved(after(source[2], held[0]), 0, 1, (1,))

    def projected(chunk, *others):
        parts = [source[chunk], source_other[chunk]]
        if chunk < 4:
            parts = [query[chunk], query_other[chunk]] + parts
        parts[0] = after(parts[0], *others)
        (kept, sent), held[0] = project(table, parts, gains, held[0], 2)
        return kept, moved(sent, 1, 0)

    done = {0: projected(0, query[2], source[2])}
    before = done[0][0]
    if seq > 4:
        source[4] = after(source[4], before)
        source_other[4] = moved(source[4], 0, 1)
    last = [before, source.get(4, before)]
    for chunk in chunks[3:]:
        source[chunk] = moved(after(source_away if chunk & 2 else source_own, last), chunk, 0)
        last = source[chunk]
    done[2] = projected(2, before)
    before = done[2][0]
    for chunk in chunks[2:]:
        if chunk > 4:
            source_other[chunk] = moved(after(source[chunk], done[2][0]), 0, 1)
        done[chunk] = projected(chunk, before, done[chunk - 4][1])
        before = done[chunk][0]
    arrays = [array for chunk in chunks for array in done[chunk]]

    lengths = lengths.reshape(-1)
    context = attend(table, lengths, arrays, (0, 1), width)
    first_context = [context[0], moved(context[1], 1, 0)]
    context = attend(table, lengths, after(arrays, context), (2, 3), width)
    second_context = [moved(after(context[turn], first_context[1]), 2 + turn, 0) for turn in range(2)]
    away, own = output_parts(table, first_context, w_out[0])
    first_beside = moved(away, 0, 1)
    away, second_own = output_parts(table, second_context, w_out[0])
    second_beside = moved(away, 0, 1)
    return add_all(table, hidden, own, first_beside, second_own, second_beside)


def solution(mesh):
    seq, mp = mesh.shape["seq"], mesh.shape["mp"]

    def chosen(*arrays):
        batch, columns = arrays[0].shape[1], arrays[2].shape[2]
        fits = (
            batch == 2
            and mp == 2
            and seq >= 4
            and seq & (seq - 1) == 0
            and (columns // mp) % (2 * LANES) == 0
            and (arrays[0].shape[2] // seq) % 16 == 0
        )
        return jax.shard_map(
            body if fits else gathered_body,
            mesh=mesh,
            in_specs=(
                P("segment", None, "seq", "mp"),
                P("segment", None, "seq", "mp"),
                P("segment", None, "mp"),
                P("segment", None, "mp"),
                P("segment", None, "mp"),
                P("segment", "mp", None),
                P("segment", None),
                P(),
                P("segment", None, None),
            ),
            out_specs=P("segment", None, "seq", "mp"),
            check_vma=False,
        )(*arrays)

    return chosen
```

```python
import functools

import jax
import jax.numpy as jnp
from jax import lax
from jax.experimental import pallas as pl
from jax.experimental.pallas import tpu as pltpu
from jax.sharding import PartitionSpec as P

DH = 64
LANES = 128
SCALE = 0.25 * 1.4426950408889634
MIB = 1024 * 1024
SMALL = pl.CostEstimate(flops=1, bytes_accessed=1, transcendentals=0)
IN_VMEM = pl.BlockSpec(memory_space=pltpu.VMEM)


def passed_along(value, axis, steps):
    count = lax.axis_size(axis)
    leading, last = (max(0, -steps), min(count, count - steps))
    return lax.ppermute(value, axis, [(source, source + steps) for source in range(leading, last)])


def normalize(values, gain_row):
    widened = values.astype(jnp.float32)
    square = jnp.mean(widened * widened, axis=-1, keepdims=True)
    return (widened * lax.rsqrt(square + 1e-06) * gain_row).astype(jnp.bfloat16)


def gathered_body(hidden, memory, w_query, w_key, w_value, w_out, norm_gain, final_gain, lengths):
    encoder_side = lax.axis_index("segment") == 0
    own_part = hidden[0]
    arrived = passed_along(memory[0], "segment", 1)
    source_part = jnp.where(encoder_side, own_part, arrived)
    query_rows, source_rows = (
        lax.all_gather(own_part, "mp", axis=2, tiled=True),
        lax.all_gather(source_part, "mp", axis=2, tiled=True),
    )
    batch = own_part.shape[0]
    row_count = own_part.shape[1]
    width = query_rows.shape[2]
    key_gain = jnp.where(encoder_side, norm_gain[0], final_gain)
    query_in = normalize(query_rows.reshape(batch * row_count, width), norm_gain[0])
    key_in = normalize(source_rows.reshape(batch * row_count, width), key_gain)
    head_cols = w_query.shape[2]
    local_heads = head_cols // DH
    queries = jnp.dot(query_in, w_query[0], preferred_element_type=jnp.float32).astype(jnp.bfloat16)
    keys = jnp.dot(key_in, w_key[0], preferred_element_type=jnp.float32).astype(jnp.bfloat16)
    values = jnp.dot(key_in, w_value[0], preferred_element_type=jnp.float32).astype(jnp.bfloat16)
    keys = keys.reshape(batch, row_count, head_cols)
    values = values.reshape(batch, row_count, head_cols)
    query_length = lengths[0, :, 0]
    key_length = lengths[0, :, 1]
    split_queries = queries.reshape(batch, row_count, local_heads, DH)
    key_piece = lax.all_gather(keys, "seq", axis=1, tiled=True)
    value_piece = lax.all_gather(values, "seq", axis=1, tiled=True)
    key_count = key_piece.shape[1]
    scores = (
        jnp.einsum(
            "bqhd,bkhd->bqhk",
            split_queries,
            key_piece.reshape(batch, key_count, local_heads, DH),
            preferred_element_type=jnp.float32,
        )
        * 0.25
    )
    visible = jnp.arange(key_count)[None, :] < key_length[:, None]
    mask = visible[:, None, None, :]
    scores = jnp.where(mask, scores, -1e30)
    largest = jnp.max(scores, axis=-1)
    exponent = jnp.where(mask, jnp.exp(scores - largest[..., None]), 0.0)
    totals = jnp.sum(exponent, axis=-1)
    weighted = jnp.einsum(
        "bqhk,bkhd->bqhd",
        exponent.astype(jnp.bfloat16),
        value_piece.reshape(batch, key_count, local_heads, DH),
        preferred_element_type=jnp.float32,
    )
    context = weighted / totals[..., None]
    positions = lax.axis_index("seq") * row_count + jnp.arange(row_count)
    live_rows = positions[None, :] < query_length[:, None]
    context = jnp.where(live_rows[:, :, None, None], context, 0.0)
    context = context.astype(jnp.bfloat16).reshape(batch * row_count, head_cols)
    partial_value = jnp.dot(context, w_out[0], preferred_element_type=jnp.float32)
    branch = lax.psum_scatter(
        partial_value.astype(jnp.bfloat16), "mp", scatter_dimension=1, tiled=True
    ).astype(jnp.float32)
    branch = branch.reshape(batch, row_count, branch.shape[1])
    return (own_part.astype(jnp.float32) + branch).astype(jnp.bfloat16)[None]


HEAD, SIDE, INNER, ENC = 0, 1, 2, 3
BLOCK = 4


def in_vmem(array):
    return pltpu.with_memory_space_constraint(array, pltpu.VMEM)


def in_hbm(array):
    return pltpu.with_memory_space_constraint(array, pltpu.HBM)


def split_kernel(table, hidden, memory, own, away, sems):
    inner = table[INNER]

    def copied(array):
        copies = [
            pltpu.make_async_copy(array.at[0, inner], own, sems.at[0]),
            pltpu.make_async_copy(array.at[0, 1 - inner], away, sems.at[1]),
        ]
        for copy in copies:
            copy.start()
        for copy in copies:
            copy.wait()

    if memory is None:
        copied(hidden)
    else:
        pl.when(table[ENC] == 1)(lambda: copied(hidden))
        pl.when(table[ENC] == 0)(lambda: copied(memory))


def split(table, hidden, memory=None):
    arrays = [hidden] if memory is None else [hidden, memory]

    def kernel(table, hidden, *rest):
        split_kernel(table, hidden, *([None] if memory is None else []), *rest)

    return pl.pallas_call(
        kernel,
        out_shape=[jax.ShapeDtypeStruct(hidden.shape[2:], jnp.bfloat16)] * 2,
        in_specs=[pl.BlockSpec(memory_space=pltpu.SMEM), pl.BlockSpec(memory_space=pltpu.HBM)]
        + [pl.BlockSpec(memory_space=pl.ANY)] * (len(arrays) - 1),
        out_specs=[IN_VMEM] * 2,
        scratch_shapes=[pltpu.SemaphoreType.DMA((2,))],
        compiler_params=pltpu.CompilerParams(vmem_limit_bytes=4 * MIB),
        cost_estimate=SMALL,
    )(table, in_hbm(hidden), *arrays[1:])


def times_gain(values, gains, side, into):
    half = values.shape[1]
    wide = values.astype(jnp.float32)
    into[...] = (wide * gains[:, pl.ds(pl.multiple_of(side * half, half), half)]).astype(jnp.bfloat16)
    return jnp.sum(wide * wide, axis=-1, keepdims=True)


def row_factor(total, features):
    return lax.rsqrt(total / features + 1e-06)


def fetch_kernel(count, *refs):
    sources, targets, sems = refs[:count], refs[count:-1], refs[-1]
    copies = [
        pltpu.make_async_copy(source.at[0], target, sems.at[n])
        for n, (source, target) in enumerate(zip(sources, targets))
    ]
    for copy in copies:
        copy.start()
    for copy in copies:
        copy.wait()


def fetch(weights):
    return pl.pallas_call(
        functools.partial(fetch_kernel, len(weights)),
        out_shape=[pltpu.VMEM(weight.shape[1:], jnp.bfloat16) for weight in weights],
        in_specs=[pl.BlockSpec(memory_space=pltpu.HBM)] * len(weights),
        out_specs=[IN_VMEM] * len(weights),
        scratch_shapes=[pltpu.SemaphoreType.DMA((len(weights),))],
        compiler_params=pltpu.CompilerParams(vmem_limit_bytes=2 * MIB),
        cost_estimate=SMALL,
    )(*[in_hbm(weight) for weight in weights])


def project_kernel(count, queried, table, *refs):
    size = 4 if queried else 2
    (gain, last_gain), weights, rest = refs[size : size + 2], refs[size + 2 : size + 5], refs[size + 5 :]
    outs, (xk, xq, fk, fq) = rest[:count], rest[-4:]
    side = table[SIDE]
    rows, half = refs[0].shape
    width = weights[0].shape[1] // count

    def fill(own, other, gains, x, f):
        total = times_gain(own, gains, side, x.at[0]) + times_gain(other, gains, 1 - side, x.at[1])
        f[...] = jnp.broadcast_to(row_factor(total, 2 * half), (rows, LANES))

    if queried:
        qo, qn, ko, kn = refs[:4]
        fill(qo[...], qn[...], gain, xq, fq)

        @pl.when(table[ENC] == 1)
        def _():
            xk[...] = xq[...]
            fk[...] = fq[...]

    else:
        ko, kn = refs[:2]

        @pl.when(table[ENC] == 1)
        def _():
            fill(ko[...], kn[...], gain, xk, fk)

    @pl.when(table[ENC] == 0)
    def _():
        fill(ko[...], kn[...], last_gain, xk, fk)

    def part(s):
        return pl.ds(pl.multiple_of(s * half, half), half)

    for n in range(3 if queried else 2):
        x, f = (xq, fq) if n == 2 else (xk, fk)
        scale = f[:, :1] * SCALE if n == 2 else f[:, :1]
        for turn in range(count - 1, -1, -1):
            columns = pl.ds(pl.multiple_of((table[HEAD] ^ turn) * width, width), width)
            total = jnp.dot(x[0], weights[n][part(side), columns], preferred_element_type=jnp.float32)
            total += jnp.dot(x[1], weights[n][part(1 - side), columns], preferred_element_type=jnp.float32)
            outs[turn][:, n * width : (n + 1) * width] = (total * scale).astype(jnp.bfloat16)


def project(table, arrays, gains, weights, count):
    rows, half = arrays[0].shape
    columns = weights[0].shape[1]
    queried = len(arrays) == 4
    width = (3 if queried else 2) * columns // count
    first = 1 + len(arrays) + 2
    products = pl.pallas_call(
        functools.partial(project_kernel, count, queried),
        out_shape=[jax.ShapeDtypeStruct((rows, width), jnp.bfloat16)] * count
        + [pltpu.VMEM(weight.shape, jnp.bfloat16) for weight in weights],
        grid_spec=pltpu.PrefetchScalarGridSpec(
            num_scalar_prefetch=1,
            grid=(1,),
            in_specs=[IN_VMEM] * (len(arrays) + 2 + len(weights)),
            out_specs=[IN_VMEM] * (count + len(weights)),
            scratch_shapes=[pltpu.VMEM((2, rows, half), jnp.bfloat16)] * 2
            + [pltpu.VMEM((rows, LANES), jnp.float32)] * 2,
        ),
        input_output_aliases={first + n: count + n for n in range(len(weights))},
        compiler_params=pltpu.CompilerParams(vmem_limit_bytes=8 * MIB),
        cost_estimate=SMALL,
    )(table, *arrays, *gains, *[in_vmem(weight) for weight in weights])
    return products[:count], products[count:]


def attend_kernel(chosen, tile, blocks, table, lengths, *refs):
    arrays, outs, (qs, ks, vs, contexts) = refs[:blocks], refs[blocks:-4], refs[-4:]
    rows, width = outs[0].shape
    pairs = width // LANES
    query_length = lengths[2 * table[INNER]]
    key_length = lengths[2 * table[INNER] + 1]
    lane = lax.broadcasted_iota(jnp.int32, (rows, LANES), 1)
    row = lax.broadcasted_iota(jnp.int32, (rows, LANES), 0)
    low = lane < DH
    zero = jnp.zeros((rows, LANES), jnp.bfloat16)
    one = jnp.ones((rows, LANES), jnp.bfloat16)
    unit = jnp.where(lane == 0, one, zero)

    def lanes(block):
        return slice(block * LANES, (block + 1) * LANES)

    for j in range(blocks):
        here = pl.ds(j * rows, rows)
        hides = jnp.logical_and(lane == 0, row + table[BLOCK + j] >= key_length)
        bias = jnp.where(hides, -1e30, 0.0).astype(jnp.bfloat16)
        for pair in range(pairs):
            key = arrays[j][:, lanes(pair)]
            value = arrays[j][:, lanes(pairs + pair)]
            ks[pair, 0, here, :LANES] = jnp.where(low, key, zero)
            ks[pair, 1, here, :LANES] = jnp.where(low, zero, key)
            ks[pair, 0, here, LANES:] = bias
            ks[pair, 1, here, LANES:] = bias
            vs[pair, 0, here, :] = jnp.where(low, value, one)
            vs[pair, 1, here, :] = jnp.where(low, one, value)
    for i, j in enumerate(chosen):
        here = pl.ds(i * rows, rows)
        for pair in range(pairs):
            qs[pair, here, :LANES] = arrays[j][:, lanes(2 * pairs + pair)]
            qs[pair, here, LANES:] = unit

    low = lax.broadcasted_iota(jnp.int32, (tile, LANES), 1) < DH
    for pair in range(pairs):
        for t in range(len(chosen) * rows // tile):
            here = pl.ds(t * tile, tile)
            sums = []
            for head in range(2):
                scores = lax.dot_general(
                    qs[pair, here, :], ks[pair, head], (((1,), (1,)), ((), ())), preferred_element_type=jnp.float32
                )
                largest = jnp.max(scores, axis=-1, keepdims=True)
                weights = jnp.exp2(scores - largest).astype(jnp.bfloat16)
                sums.append(jnp.dot(weights, vs[pair, head], preferred_element_type=jnp.float32))
            weighted = jnp.where(low, sums[0], sums[1])
            totals = jnp.where(low, pltpu.roll(sums[0], DH, 1), pltpu.roll(sums[1], DH, 1))
            contexts[here, lanes(pair)] = (weighted / totals).astype(jnp.bfloat16)

    for i, j in enumerate(chosen):
        live = row + table[BLOCK + j] < query_length
        for pair in range(pairs):
            outs[i][:, lanes(pair)] = jnp.where(live, contexts[pl.ds(i * rows, rows), lanes(pair)], zero)


def attend(table, lengths, arrays, chosen, width):
    rows = arrays[0].shape[0]
    total = len(arrays) * rows
    size = len(chosen) * rows
    pairs = width // LANES
    return pl.pallas_call(
        functools.partial(attend_kernel, chosen, size, len(arrays)),
        out_shape=[jax.ShapeDtypeStruct((rows, width), jnp.bfloat16)] * len(chosen),
        grid_spec=pltpu.PrefetchScalarGridSpec(
            num_scalar_prefetch=2,
            grid=(1,),
            in_specs=[IN_VMEM] * len(arrays),
            out_specs=[IN_VMEM] * len(chosen),
            scratch_shapes=[
                pltpu.VMEM((pairs, size, 2 * LANES), jnp.bfloat16),
                pltpu.VMEM((pairs, 2, total, 2 * LANES), jnp.bfloat16),
                pltpu.VMEM((pairs, 2, total, LANES), jnp.bfloat16),
                pltpu.VMEM((size, width), jnp.bfloat16),
            ],
        ),
        compiler_params=pltpu.CompilerParams(vmem_limit_bytes=32 * MIB),
        cost_estimate=SMALL,
    )(table, lengths, *arrays)


def output_kernel(count, table, w, *refs):
    pieces, outs, x = refs[:count], refs[count : count + 2], refs[-1]
    width = pieces[0].shape[1]
    half = outs[0].shape[1]
    for turn in range(count):
        place = pl.multiple_of((table[HEAD] ^ turn) * width, width)
        x[:, pl.ds(place, width)] = pieces[turn][...]
    for i in range(2):
        columns = pl.ds(pl.multiple_of((1 - (table[SIDE] ^ i)) * half, half), half)
        outs[i][...] = jnp.dot(x[...], w[:, columns], preferred_element_type=jnp.float32).astype(jnp.bfloat16)


def output_parts(table, pieces, w_out):
    rows, width = pieces[0].shape
    depth, half = w_out.shape[0], w_out.shape[1] // 2
    return pl.pallas_call(
        functools.partial(output_kernel, len(pieces)),
        out_shape=[jax.ShapeDtypeStruct((rows, half), jnp.bfloat16)] * 2,
        grid_spec=pltpu.PrefetchScalarGridSpec(
            num_scalar_prefetch=1,
            grid=(1,),
            in_specs=[IN_VMEM] * (1 + len(pieces)),
            out_specs=[IN_VMEM] * 2,
            scratch_shapes=[pltpu.VMEM((rows, depth), jnp.bfloat16)],
        ),
        compiler_params=pltpu.CompilerParams(vmem_limit_bytes=16 * MIB),
        cost_estimate=SMALL,
    )(table, w_out, *pieces)


def add_kernel(table, hidden, own, beside, across, corner, out):
    def total(a, b):
        out[0, 0] = (
            hidden[0, 0].astype(jnp.float32) + (a[...].astype(jnp.float32) + b[...].astype(jnp.float32))
        ).astype(jnp.bfloat16)

    @pl.when(pl.program_id(0) == 0)
    def _():
        total(own, beside)

    @pl.when(pl.program_id(0) == 1)
    def _():
        total(across, corner)


def add_all(table, hidden, own, beside, across, corner):
    rows, half = own.shape
    block = pl.BlockSpec((1, 1, rows, half), lambda i, table: (0, table[INNER] ^ i, 0, 0))
    part = pl.BlockSpec((rows, half), lambda i, table: (0, 0))
    return pl.pallas_call(
        add_kernel,
        out_shape=jax.ShapeDtypeStruct(hidden.shape, jnp.bfloat16),
        grid_spec=pltpu.PrefetchScalarGridSpec(
            num_scalar_prefetch=1,
            grid=(2,),
            in_specs=[block, part, part, part, part],
            out_specs=block,
        ),
        compiler_params=pltpu.CompilerParams(vmem_limit_bytes=16 * MIB),
    )(table, hidden, own, beside, across, corner)


def body(hidden, memory, w_query, w_key, w_value, w_out, norm_gain, final_gain, lengths):
    seq, mp = lax.axis_size("seq"), lax.axis_size("mp")
    width = w_query.shape[2] // 2
    rows = hidden.shape[2]

    place, side = lax.axis_index("seq"), lax.axis_index("mp")
    encoder = (lax.axis_index("segment") == 0).astype(jnp.int32)
    chunks = range(0, seq, 2)
    starts = [(place ^ (chunk + turn)) * rows for chunk in chunks for turn in range(2)]
    table = jnp.stack([place % 2, side, place // 2 % 2, encoder] + starts).astype(jnp.int32)

    def moved(value, swap_seq, swap_mp, segments=(0, 1)):
        pairs = [
            ((g * seq + s) * mp + m, (g * seq + (s ^ swap_seq)) * mp + (m ^ swap_mp))
            for g in segments
            for s in range(seq)
            for m in range(mp)
        ]
        return lax.ppermute(value, ("segment", "seq", "mp"), pairs)

    def after(value, *others):
        return lax.optimization_barrier((value, *others))[0]

    gains = (in_hbm(norm_gain), in_hbm(final_gain.reshape(1, -1)))
    weights = (w_key, w_value, w_query)

    arrived = passed_along(memory[0], "segment", 1)
    hidden_own, hidden_away = split(table, hidden)
    query = {0: hidden_own}
    query_other = {0: moved(hidden_own, 0, 1)}
    query[2] = moved(hidden_away, 2, 0)
    source_own, source_away = split(table, hidden, after(arrived, hidden_own)[None])
    source = {0: source_own}
    source_other = {0: moved(source_own, 0, 1, (1,))}
    source[2] = moved(source_away, 2, 0, (1,))
    if seq > 4:
        source[4] = moved(after(source_own, query_other[0]), 4, 0)
    held = [fetch([after(weight, query_other[0]) for weight in weights])]
    query_other[2] = moved(after(query[2], held[0]), 0, 1)
    source_other[2] = moved(after(source[2], held[0]), 0, 1, (1,))

    def projected(chunk, *others):
        parts = [source[chunk], source_other[chunk]]
        if chunk < 4:
            parts = [query[chunk], query_other[chunk]] + parts
        parts[0] = after(parts[0], *others)
        (kept, sent), held[0] = project(table, parts, gains, held[0], 2)
        return kept, moved(sent, 1, 0)

    done = {0: projected(0)}
    before = done[0][0]
    if seq > 4:
        source[4] = after(source[4], before)
        source_other[4] = moved(source[4], 0, 1)
    last = [before, source.get(4, before)]
    for chunk in chunks[3:]:
        source[chunk] = moved(after(source_away if chunk & 2 else source_own, last), chunk, 0)
        last = source[chunk]
    done[2] = projected(2, before)
    before = done[2][0]
    for chunk in chunks[2:]:
        if chunk > 4:
            source_other[chunk] = moved(after(source[chunk], done[2][0]), 0, 1)
        done[chunk] = projected(chunk, before, done[chunk - 4][1])
        before = done[chunk][0]
    arrays = [array for chunk in chunks for array in done[chunk]]

    lengths = lengths.reshape(-1)
    context = attend(table, lengths, arrays, (0, 1), width)
    first_context = [context[0], moved(context[1], 1, 0)]
    context = attend(table, lengths, after(arrays, context), (2, 3), width)
    second_context = [moved(after(context[turn], first_context[1]), 2 + turn, 0) for turn in range(2)]
    away, own = output_parts(table, first_context, w_out[0])
    first_beside = moved(away, 0, 1)
    away, second_own = output_parts(table, second_context, w_out[0])
    second_beside = moved(away, 0, 1)
    return add_all(table, hidden, own, first_beside, second_own, second_beside)


def solution(mesh):
    seq, mp = mesh.shape["seq"], mesh.shape["mp"]

    def chosen(*arrays):
        batch, columns = arrays[0].shape[1], arrays[2].shape[2]
        fits = (
            batch == 2
            and mp == 2
            and seq >= 4
            and seq & (seq - 1) == 0
            and (columns // mp) % (2 * LANES) == 0
            and (arrays[0].shape[2] // seq) % 16 == 0
        )
        return jax.shard_map(
            body if fits else gathered_body,
            mesh=mesh,
            in_specs=(
                P("segment", None, "seq", "mp"),
                P("segment", None, "seq", "mp"),
                P("segment", None, "mp"),
                P("segment", None, "mp"),
                P("segment", None, "mp"),
                P("segment", "mp", None),
                P("segment", None),
                P(),
                P("segment", None, None),
            ),
            out_specs=P("segment", None, "seq", "mp"),
            check_vma=False,
        )(*arrays)

    return chosen
```
